128 devices in a mesh: dp: 16 (over x, z_lo, core), expert: 8 (over z_hi, y).
Axes of the slice: x: 4, y: 4, z: 4 (z_hi: 2, z_lo: 2; z = z_hi * 2 + z_lo), core: 2. Of those that a mesh axis runs over, the one named last changes fastest.
Arguments:
- tokens: bfloat16 [1024, 256, 1280], P(('dp', 'expert')), may hold values from -80 to 80
- router: bfloat16 [1280, 16], replicated, may hold values from -1 to 1
- weight_in: bfloat16 [16, 1280, 5120], P('expert', None, 'dp'), may hold values from -0.15625 to 0.15625
- weight_out: bfloat16 [16, 5120, 1280], P('expert', 'dp'), may hold values from -0.078125 to 0.078125
- out_grad: bfloat16 [1024, 256, 1280], P(('dp', 'expert')), may hold values from -6 to 6
Outputs:
- token_grad: bfloat16 [1024, 256, 1280], P(('dp', 'expert'))
- router_grad: float32 [1280, 16], replicated
- weight_in_grad: bfloat16 [16, 1280, 5120], P('expert', None, 'dp')
- weight_out_grad: bfloat16 [16, 5120, 1280], P('expert', 'dp')
The draws below stay inside these ranges and needn't reach their ends.
All inputs are finite; a program needn't handle non-finite values.
Results may differ from the reference program's by a relative error of at most 0.03.
Values may be sent and summed in bfloat16 or wider, within the bound.
A program may use at most 128 MiB of HBM per device.

```python
import math
import jax
import jax.numpy as jnp
from jax import lax

D = 1280
FF = 5120
M = 256
EXPERTS = 16
IMAGES = 1024
N_DP = 16


def common_basis(key):
    return jnp.clip(jax.random.normal(key, (D, EXPERTS), jnp.float32), -4.0, 4.0)


def draw_router(key, part):
    basis = common_basis(key)
    return (basis / math.sqrt(D)).astype(jnp.bfloat16)


def draw_tokens(key, part):
    key = jax.random.fold_in(key, 7)
    first_key = jax.random.fold_in(key, 0)
    return jax.random.normal(first_key, (IMAGES, M, D), jnp.float32).astype(jnp.bfloat16)


def steps_of(own_key, shape, shards, least, top_value):
    def one(position, parts):
        steps = jax.random.uniform(jax.random.fold_in(jax.random.fold_in(own_key, 6), position), (parts,), jnp.float32, least / len(shards), top_value / len(shards))
        return jnp.repeat(jnp.exp(steps), shape[position] // parts).reshape((-1,) + (1,) * (len(shape) - position - 1))

    gain = one(*shards[0])
    for cut in shards[1:]:
        gain = gain * one(*cut)
    return gain


def centred(own_key, shape, scale, limit, pieces=(), dtype=jnp.bfloat16):
    loudness = steps_of(own_key, shape, pieces, -0.22, 0.18) if pieces else 1.0
    values = jax.random.normal(own_key, shape, jnp.float32) * scale * loudness
    return jnp.minimum(jnp.maximum(values, -limit), limit).astype(dtype)


def setup_inputs(seed: int = 0) -> dict:
    splits = jax.random.split(jax.random.key(seed), 6)
    return {
        "tokens": draw_tokens(jax.random.fold_in(splits[5], 71), 0),
        "router": draw_router(jax.random.fold_in(splits[5], 71), 0),
        "weight_in": centred(splits[2], (EXPERTS, D, FF), D ** -0.5, 0.15625, ((0, 8), (2, 16))),
        "weight_out": centred(splits[3], (EXPERTS, FF, D), FF ** -0.5, 0.078125, ((0, 8), (1, 16))),
        "out_grad": centred(splits[4], (IMAGES, M, D), 1.0, 6.0, ((0, 128),)),
    }


root_half = 0.7071067811865476
inv_root_tau = 0.3989422804014327


def fdot(left, right):
    return jnp.dot(left.astype(jnp.float32), right.astype(jnp.float32), precision=lax.Precision.HIGHEST)


def gelu_value(hidden):
    return 0.5 * hidden * (1.0 + jax.scipy.special.erf(hidden * root_half))


def gelu_slope(hidden):
    return 0.5 * (1.0 + jax.scipy.special.erf(hidden * root_half)) + hidden * jnp.exp(-0.5 * hidden * hidden) * inv_root_tau


def route_image(image, router):
    logits = fdot(image, router).T
    dispatch = jax.nn.softmax(logits, axis=1)
    combine = jax.nn.softmax(logits, axis=0)
    return dispatch, combine


def grouped_sum(partial_value):
    rounded = lax.optimization_barrier(partial_value.astype(jnp.bfloat16))
    return jnp.sum(rounded.astype(jnp.float32), axis=1).astype(jnp.bfloat16)


def expert_pass(slot_rows, grad_rows, weight_in, weight_out):
    per_group = FF // N_DP
    hidden = fdot(slot_rows, weight_in)
    active = gelu_value(hidden).astype(jnp.bfloat16)
    active_groups = active.reshape(IMAGES, N_DP, per_group).astype(jnp.float32)
    out_pieces = weight_out.reshape(N_DP, per_group, D).astype(jnp.float32)
    slot_out = grouped_sum(jnp.einsum('rgf,gfd->rgd', active_groups, out_pieces, precision=lax.Precision.HIGHEST))
    grad_act = fdot(grad_rows, weight_out.T)
    grad_hidden = (grad_act * gelu_slope(hidden)).astype(jnp.bfloat16)
    weight_out_grad = fdot(active.T, grad_rows).astype(jnp.bfloat16)
    weight_in_grad = fdot(slot_rows.T, grad_hidden).astype(jnp.bfloat16)
    hidden_groups = grad_hidden.reshape(IMAGES, N_DP, per_group).astype(jnp.float32)
    in_pieces = weight_in.reshape(D, N_DP, per_group).astype(jnp.float32)
    slot_back = grouped_sum(jnp.einsum('rgf,dgf->rgd', hidden_groups, in_pieces, precision=lax.Precision.HIGHEST))
    return slot_out, slot_back, weight_in_grad, weight_out_grad


def reference(tokens, router, weight_in, weight_out, out_grad):
    def slot_pair(pair):
        image, grad_image = pair
        dispatch, combine = route_image(image, router)
        slot_in = fdot(dispatch.astype(jnp.bfloat16), image).astype(jnp.bfloat16)
        slot_grad = fdot(combine.astype(jnp.bfloat16), grad_image).astype(jnp.bfloat16)
        return slot_in, slot_grad

    slot_in, slot_grad = lax.map(slot_pair, (tokens, out_grad))

    def run_expert(group):
        return expert_pass(group[0], group[1], group[2], group[3])

    slot_out_t, slot_back_t, weight_in_grad, weight_out_grad = lax.map(
        run_expert, (jnp.swapaxes(slot_in, 0, 1), jnp.swapaxes(slot_grad, 0, 1), weight_in, weight_out))
    slot_out = jnp.swapaxes(slot_out_t, 0, 1)
    slot_back = jnp.swapaxes(slot_back_t, 0, 1)

    def image_grads(router_total, group):
        image, grad_image, image_out, image_back = group
        dispatch, combine = route_image(image, router)
        grad_comb = fdot(image_out, grad_image.T)
        comb_logit = combine * (grad_comb - jnp.sum(combine * grad_comb, axis=0, keepdims=True))
        grad_disp = fdot(image_back, image.T)
        disp_logit = dispatch * (grad_disp - jnp.sum(dispatch * grad_disp, axis=1, keepdims=True))
        logit_grad = (comb_logit + disp_logit).astype(jnp.bfloat16)
        token_part = fdot(dispatch.astype(jnp.bfloat16).T, image_back)
        token_part = token_part + fdot(logit_grad.T, router.T)
        router_total = router_total + fdot(image.T, logit_grad.T)
        return router_total, token_part.astype(jnp.bfloat16)

    router_grad, token_grad = lax.scan(image_grads, jnp.zeros((D, EXPERTS), jnp.float32),
                                       (tokens, out_grad, slot_out, slot_back))
    return token_grad, router_grad, weight_in_grad, weight_out_grad
```

```python
import jax
import jax.numpy as jnp
from jax import lax
from jax.experimental import pallas as pl
from jax.experimental.pallas import tpu as pltpu
from jax.sharding import PartitionSpec as P

MESH = pl.DeviceIdType.MESH
BF = jnp.bfloat16
F32 = jnp.float32

D = 1280
M = 256
S = 16
IMG = 8
HID = 320
HID2 = 640
ROWS = 512

root_half = 0.7071067811865476
inv_root_tau = 0.3989422804014327

NT = (((1,), (1,)), ((), ()))
TN = (((0,), (0,)), ((), ()))


def dot(a, b):
    return jnp.dot(a, b, preferred_element_type=F32)


def dot_nt(a, b):
    return lax.dot_general(a, b, NT, preferred_element_type=F32)


def dot_tn(a, b):
    return lax.dot_general(a, b, TN, preferred_element_type=F32)


def permute_rows(source_of, value):
    r = lax.broadcasted_iota(jnp.int32, (128, 128), 0)
    c = lax.broadcasted_iota(jnp.int32, (128, 128), 1)
    matrix = jnp.where(c == source_of(r), 1.0, 0.0).astype(BF)
    return dot(matrix, value).astype(BF)


def by_slot(r):
    return (r & 7) * 16 + (r >> 3)


def by_image(r):
    return (r & 15) * 8 + (r >> 4)


def by_expert(r):
    return ((r >> 3) & 7) * 16 + (r >> 6) * 8 + (r & 7)


def by_peer(r):
    return ((r >> 3) & 1) * 64 + (r >> 4) * 8 + (r & 7)


def rows16(index):
    return pl.ds(pl.multiple_of(index * 16, 16), 16)


def kernel(
    tok_h, grad_h, rt_ref, w1_h, w2_h,
    token_grad_h, router_out, dw1_h, dw2_h,
    tok, grad, w1, w2, disp, comb, stage, a2a_s, a2a_r, rows, parts, rsb,
    hid, act, act_t, dwk, dws, dwr, fin, back_s, back_r, sb, lg, tgo,
    arp, arr, ars, arg, arf,
    s_load, s_w, s_wr, s_a2a, r_a2a, s_ag, r_ag, s_rs, r_rs, s_bk, r_bk,
    s_dw, r_dw, s_out, s_dwo, s_ar1, r_ar1, s_ar2, r_ar2, s_ar3, r_ar3, s_loc,
):
    dp = lax.axis_index("dp")
    ex = lax.axis_index("expert")
    x, zl, core = dp // 4, (dp // 2) % 2, dp % 2
    zh, y = ex // 4, ex % 4

    def in_dp(dx, dz, dc=0):
        return (((x + dx) % 4) * 4 + ((zl + dz) % 2) * 2 + (core + dc) % 2, ex)

    def ex_of(k, sign=1):
        return ((zh + k // 4) % 2) * 4 + (y + 4 + sign * (k % 4)) % 4

    def remote(src, dst, s_sem, r_sem, device):
        return pltpu.make_async_remote_copy(
            src_ref=src, dst_ref=dst, send_sem=s_sem, recv_sem=r_sem,
            device_id=device, device_id_type=MESH,
        )

    barrier = pltpu.get_barrier_semaphore()
    for n in range(1, 16):
        pl.semaphore_signal(
            barrier, inc=1, device_id=in_dp(n // 4, (n // 2) % 2, n % 2), device_id_type=MESH
        )
    for k in range(1, 8):
        pl.semaphore_signal(barrier, inc=1, device_id=(dp, ex_of(k)), device_id_type=MESH)

    def load(which, i):
        src, dst = ((tok_h, tok), (grad_h, grad))[which]
        return pltpu.make_async_copy(src.at[i], dst.at[i], s_load.at[which, i])

    for which in range(2):
        for i in range(IMG):
            load(which, i).start()
    own_w = []
    for j in range(2):
        for n, (src, dst) in enumerate(((w1_h, w1), (w2_h, w2))):
            own_w.append(pltpu.make_async_copy(
                src.at[j], dst.at[j, pl.ds(0, HID)], s_loc.at[n, j]))
    for cp in own_w:
        cp.start()

    rt = rt_ref[...]

    def pre_in(i, carry):
        load(0, i).wait()
        image = tok[i]
        logits = dot_nt(rt, image)
        e1 = jnp.exp(logits - jnp.max(logits, axis=1, keepdims=True))
        d = e1 / jnp.sum(e1, axis=1, keepdims=True)
        e0 = jnp.exp(logits - jnp.max(logits, axis=0, keepdims=True))
        c = e0 / jnp.sum(e0, axis=0, keepdims=True)
        disp[i] = d
        comb[i] = c
        stage[rows16(i)] = dot(d.astype(BF), image).astype(BF)
        return carry

    def pre_grad(i, carry):
        load(1, i).wait()
        stage[rows16(i)] = dot(comb[i].astype(BF), grad[i]).astype(BF)
        return carry

    def start_a2a(a):
        a2a_s[a] = permute_rows(by_slot, stage[...])
        cps = []
        for k in range(1, 8):
            cp = remote(
                a2a_s.at[a, rows16(ex_of(k))], a2a_r.at[a, pl.ds(k * 16, 16)],
                s_a2a.at[a, k], r_a2a.at[a, k], (dp, ex_of(k)),
            )
            cp.start()
            cps.append(cp)
        a2a_r[a, pl.ds(0, 16)] = a2a_s[a, rows16(ex)]
        return cps

    lax.fori_loop(0, IMG, pre_in, 0)
    pl.semaphore_wait(barrier, 22)
    a2a = [start_a2a(0)]
    far_w = []
    for n, (src, dst) in enumerate(((w1_h, w1), (w2_h, w2))):
        for j in range(2):
            cp = remote(
                src.at[j], dst.at[j, pl.ds(HID, HID)], s_w.at[n, j], s_wr.at[n, j], in_dp(0, 0, 1)
            )
            cp.start()
            far_w.append(cp)
    lax.fori_loop(0, IMG, pre_grad, 0)
    a2a.append(start_a2a(1))

    ag = {}

    def ag_copy(a, j, src_slot, dst_slot, dx, dz):
        cp = remote(
            rows.at[a, j, pl.ds(src_slot * 64, 64)], rows.at[a, j, pl.ds(dst_slot * 64, 64)],
            s_ag.at[a, j, dst_slot], r_ag.at[a, j, dst_slot], in_dp(dx, dz),
        )
        cp.start()
        ag[a, j, dst_slot] = cp

    def ag_begin(a):
        for cp in a2a[a]:
            cp.wait_recv()
        ordered = permute_rows(by_expert, a2a_r[a])
        for j in range(2):
            rows[a, j, pl.ds(0, 64)] = ordered[j * 64 : j * 64 + 64]
        ag_copy(a, 0, 0, 1, 0, 1)
        for dx in (1, 3, 2):
            for j in range(2):
                ag_copy(a, j, 0, 2 * dx, dx, 0)
        ag_copy(a, 1, 0, 1, 0, 1)

    def ag_forward(a):
        ag[a, 0, 1].wait_recv()
        for dx in (1, 3, 2):
            ag_copy(a, 0, 1, 2 * dx + 1, dx, 0)
        for dx in (1, 3, 2):
            ag[a, 1, 2 * dx].wait_recv()
            ag_copy(a, 1, 2 * dx, 2 * dx + 1, 0, 1)

    def ag_end(a, j):
        skip = (1,) if j == 0 else (2, 4, 6)
        for slot in range(1, 8):
            if slot not in skip:
                ag[a, j, slot].wait_recv()

    def project(a, w, j, finish):
        for h in range(2):
            hid[j, pl.ds(h * 256, 256)] = finish(
                j, h, dot_nt(rows[a, j, pl.ds(h * 256, 256)], w[j]))

    def keep(j, h, value):
        return value

    def gelu(j):
        def step(n, carry):
            at = pl.ds(pl.multiple_of(n * 32, 32), 32)
            v = hid[j, at]
            half = 0.5 * (1.0 + lax.erf(v * root_half))
            act[j, at] = (v * half).astype(BF)
            hid[j, at] = half + v * jnp.exp(-0.5 * v * v) * inv_root_tau
            return carry

        lax.fori_loop(0, ROWS // 32, step, 0)

    def slope(j, h, value):
        return value * hid[j, pl.ds(h * 256, 256)]

    def to_parts(o, w, j):
        def step(n, carry):
            at = pl.ds(pl.multiple_of(n * 256, 256), 256)
            parts[o, j, :, at] = dot(act[j], w[j, :, at]).astype(BF)
            return carry

        lax.fori_loop(0, D // 256, step, 0)

    dw = []

    def weight_grad(n, a, j):
        def step(m, carry):
            at = pl.ds(pl.multiple_of(m * 256, 256), 256)
            total = dot(act_t[...], rows[a, j, :, at])
            dwk[n, j, :, at] = total[:HID]
            dws[n, j, :, at] = total[HID:].astype(BF)
            return carry

        lax.fori_loop(0, D // 256, step, 0)
        cp = remote(dws.at[n, j], dwr.at[n, j], s_dw.at[n, j], r_dw.at[n, j], in_dp(0, 0, 1))
        cp.start()
        dw.append((cp, n, j))

    rs = {}

    def rs_copy(o, j, slot, land, dx, dz):
        cp = remote(
            parts.at[o, j, pl.ds(slot * 64, 64)], rsb.at[o, j, land],
            s_rs.at[o, j, land], r_rs.at[o, j, land], in_dp(dx, dz),
        )
        cp.start()
        rs[o, j, land] = cp

    def rs_begin(o, j):
        if j == 0:
            for dx in (2, 1, 3):
                for dz in (1, 0):
                    rs_copy(o, j, 2 * dx + dz, 2 * (dx - 1) + dz, 4 - dx, 0)
        else:
            for dx in (2, 1, 3, 0):
                rs_copy(o, j, 2 * dx + 1, dx, 0, 1)

    def part(o, j, slot):
        return parts[o, j, pl.ds(slot * 64, 64)].astype(F32)

    def landed(o, j, land):
        rs[o, j, land].wait_recv()
        return rsb[o, j, land].astype(F32)

    def rs_middle(o, j):
        if j == 0:
            total = part(o, j, 1)
            for dx in (1, 3, 2):
                total = total + landed(o, j, 2 * (dx - 1) + 1)
            parts[o, j, pl.ds(64, 64)] = total.astype(BF)
            rs_copy(o, j, 1, 6, 0, 1)
        else:
            for dx in (2, 1, 3):
                total = part(o, j, 2 * dx) + landed(o, j, dx)
                parts[o, j, pl.ds(128 * dx, 64)] = total.astype(BF)
                rs_copy(o, j, 2 * dx, 3 + dx, 4 - dx, 0)

    def rs_end(o, j):
        total = part(o, j, 0)
        if j == 0:
            lands = (0, 4, 2, 6)
        else:
            lands = (0, 4, 6, 5)
        for land in lands:
            total = total + landed(o, j, land)
        fin[pl.ds(64 * j, 64)] = total.astype(BF)

    def give_back(o):
        back_s[o] = permute_rows(by_peer, fin[...])
        cps = []
        for k in range(1, 8):
            cp = remote(
                back_s.at[o, pl.ds(k * 16, 16)], back_r.at[o, rows16(ex)],
                s_bk.at[o, k], r_bk.at[o, k], (dp, ex_of(k, -1)),
            )
            cp.start()
            cps.append(cp)
        back_r[o, rows16(ex)] = back_s[o, pl.ds(0, 16)]
        return cps

    def take_back(o, cps):
        for cp in cps:
            cp.wait_recv()
        return permute_rows(by_image, back_r[o])

    ag_begin(0)
    ag_begin(1)
    ag_forward(0)
    for cp in own_w:
        cp.wait()
    for cp in far_w:
        cp.wait_recv()
    for j in range(2):
        ag_end(0, j)
        project(0, w1, j, keep)
        if j == 0:
            ag_forward(1)
        gelu(j)
        to_parts(0, w2, j)
        rs_begin(0, j)
    for j in range(2):
        ag_end(1, j)
        act_t[...] = act[j].T
        weight_grad(1, 1, j)
        project(1, w2, j, slope)
        act[j] = hid[j].astype(BF)
        to_parts(1, w1, j)
        rs_begin(1, j)
        if j == 0:
            rs_middle(0, 0)
        act_t[...] = act[j].T
        weight_grad(0, 0, j)
    rs_middle(0, 1)
    rs_end(0, 0)
    rs_end(0, 1)
    backs = [give_back(0)]
    rs_middle(1, 0)
    rs_middle(1, 1)

    for cp, n, j in dw:
        cp.wait()
        dws[n, j] = (dwk[n, j] + dwr[n, j].astype(F32)).astype(BF)
        out = (dw1_h, dw2_h)[n]
        pltpu.make_async_copy(dws.at[n, j], out.at[j], s_dwo.at[n, j]).start()

    sb[0] = take_back(0, backs[0])

    def comb_side(i, carry):
        g = dot_nt(sb[0, rows16(i)], grad[i])
        c = comb[i]
        comb[i] = c * (g - jnp.sum(c * g, axis=0, keepdims=True))
        return carry

    lax.fori_loop(0, IMG, comb_side, 0)

    rs_end(1, 0)
    rs_end(1, 1)
    backs.append(give_back(1))
    sb[1] = take_back(1, backs[1])

    def disp_side(i, total):
        g = dot_nt(sb[1, rows16(i)], tok[i])
        d = disp[i]
        grad_logit = (comb[i] + d * (g - jnp.sum(d * g, axis=1, keepdims=True))).astype(BF)
        lg[i] = grad_logit
        return total + dot(grad_logit, tok[i])

    term = lax.fori_loop(0, IMG, disp_side, jnp.zeros((S, D), F32))
    for p in range(8):
        lane = 384 * (p // 2)
        width = min(384, D - lane)
        arp[p, :, pl.ds(0, width)] = term[8 * (p % 2) : 8 * (p % 2) + 8, lane : lane + width]
        if width < 384:
            arp[p, :, pl.ds(width, 384 - width)] = jnp.zeros((8, 384 - width), F32)

    ar1 = []
    for k in range(1, 8):
        cp = remote(arp.at[ex_of(k)], arr.at[k], s_ar1.at[k], r_ar1.at[k], (dp, ex_of(k)))
        cp.start()
        ar1.append(cp)

    def out_copy(i):
        return pltpu.make_async_copy(tgo.at[i % 2], token_grad_h.at[i], s_out.at[i])

    def token_side(first, last):
        for i in range(first, last):
            if i >= 2:
                out_copy(i - 2).wait()
            left = jnp.concatenate([disp[i].astype(BF), lg[i]], axis=0)
            right = jnp.concatenate([sb[1, pl.ds(i * 16, 16)], rt], axis=0)
            tgo[i % 2] = dot_tn(left, right).astype(BF)
            out_copy(i).start()

    token_side(0, 3)
    total = arp[ex]
    for k, cp in enumerate(ar1, 1):
        cp.wait_recv()
        total = total + arr[k]
    ars[...] = total
    ar2 = []
    for n in range(1, 16):
        cp = remote(
            ars, arg.at[dp], s_ar2.at[n], r_ar2.at[n], in_dp(n // 4, (n // 2) % 2, n % 2))
        cp.start()
        ar2.append(cp)
    arg[dp] = total
    token_side(3, 6)
    for cp in ar2:
        cp.wait_recv()
    total = arg[0]
    for n in range(1, 16):
        total = total + arg[n]
    for cp in ar2:
        cp.wait_send()
    ars[...] = total
    ar3 = []
    for k in range(1, 8):
        cp = remote(ars, arf.at[ex], s_ar3.at[k], r_ar3.at[k], (dp, ex_of(k)))
        cp.start()
        ar3.append(cp)
    arf[ex] = total
    token_side(6, 8)
    for cp in ar3:
        cp.wait()
    for p in range(8):
        lane = 384 * (p // 2)
        width = min(384, D - lane)
        router_out[pl.ds(8 * (p % 2), 8), pl.ds(lane, width)] = arf[p, :, pl.ds(0, width)]

    out_copy(6).wait()
    out_copy(7).wait()
    for n in range(2):
        for j in range(2):
            out = (dw1_h, dw2_h)[n]
            pltpu.make_async_copy(dws.at[n, j], out.at[j], s_dwo.at[n, j]).wait()
    for group in (a2a[0], a2a[1], far_w, ag.values(), rs.values(), backs[0], backs[1], ar1):
        for cp in group:
            cp.wait_send()


def shards(tokens, router, weight_in, weight_out, out_grad):
    any_space = pl.BlockSpec(memory_space=pl.ANY)
    vmem = pl.BlockSpec(memory_space=pltpu.VMEM)
    dma = pltpu.SemaphoreType.DMA
    V = pltpu.VMEM
    token_grad, router_grad, dw1, dw2 = pl.pallas_call(
        kernel,
        name="soft_moe",
        out_shape=(
            jax.ShapeDtypeStruct((IMG, M, D), BF),
            jax.ShapeDtypeStruct((S, D), F32),
            jax.ShapeDtypeStruct((2, HID, D), BF),
            jax.ShapeDtypeStruct((2, HID, D), BF),
        ),
        in_specs=[any_space, any_space, vmem, any_space, any_space],
        out_specs=(any_space, vmem, any_space, any_space),
        scratch_shapes=[
            V((IMG, M, D), BF), V((IMG, M, D), BF),
            V((2, HID2, D), BF), V((2, HID2, D), BF),
            V((IMG, S, M), F32), V((IMG, S, M), F32),
            V((128, D), BF), V((2, 128, D), BF), V((2, 128, D), BF),
            V((2, 2, ROWS, D), BF), V((2, 2, ROWS, D), BF),
            V((2, 2, 7, 64, D), BF),
            V((2, ROWS, HID2), F32), V((2, ROWS, HID2), BF), V((HID2, ROWS), BF),
            V((2, 2, HID, D), F32), V((2, 2, HID, D), BF), V((2, 2, HID, D), BF),
            V((128, D), BF), V((2, 128, D), BF), V((2, 128, D), BF),
            V((2, 128, D), BF), V((IMG, S, M), BF), V((2, M, D), BF),
            V((8, 8, 384), F32), V((8, 8, 384), F32), V((8, 384), F32),
            V((16, 8, 384), F32), V((8, 8, 384), F32),
            dma((2, IMG)), dma((2, 2)), dma((2, 2)), dma((2, 8)), dma((2, 8)),
            dma((2, 2, 8)), dma((2, 2, 8)), dma((2, 2, 7)), dma((2, 2, 7)),
            dma((2, 8)), dma((2, 8)), dma((2, 2)), dma((2, 2)), dma((IMG,)), dma((2, 2)),
            dma((8,)), dma((8,)), dma((16,)), dma((16,)), dma((8,)), dma((8,)), dma((2, 2)),
        ],
        compiler_params=pltpu.CompilerParams(
            collective_id=0, has_side_effects=True, vmem_limit_bytes=62 * 2**20
        ),
    )(tokens, out_grad, router.T, jnp.swapaxes(weight_in, 1, 2), weight_out)
    return token_grad, router_grad.T, jnp.swapaxes(dw1, 1, 2), dw2


def solution(mesh):
    in_specs = (
        P(("dp", "expert"), None, None),
        P(),
        P("expert", None, "dp"),
        P("expert", "dp", None),
        P(("dp", "expert"), None, None),
    )
    out_specs = (
        P(("dp", "expert"), None, None),
        P(),
        P("expert", None, "dp"),
        P("expert", "dp", None),
    )
    return jax.shard_map(shards, mesh=mesh, in_specs=in_specs, out_specs=out_specs, check_vma=False)
```

```python
import jax
import jax.numpy as jnp
from jax import lax
from jax.experimental import pallas as pl
from jax.experimental.pallas import tpu as pltpu
from jax.sharding import PartitionSpec as P

MESH = pl.DeviceIdType.MESH
BF = jnp.bfloat16
F32 = jnp.float32

D = 1280
M = 256
S = 16
IMG = 8
HID = 320
HID2 = 640
ROWS = 512

root_half = 0.7071067811865476
inv_root_tau = 0.3989422804014327

NT = (((1,), (1,)), ((), ()))
TN = (((0,), (0,)), ((), ()))


def dot(a, b):
    return jnp.dot(a, b, preferred_element_type=F32)


def dot_nt(a, b):
    return lax.dot_general(a, b, NT, preferred_element_type=F32)


def dot_tn(a, b):
    return lax.dot_general(a, b, TN, preferred_element_type=F32)


def permute_rows(source_of, value):
    r = lax.broadcasted_iota(jnp.int32, (128, 128), 0)
    c = lax.broadcasted_iota(jnp.int32, (128, 128), 1)
    matrix = jnp.where(c == source_of(r), 1.0, 0.0).astype(BF)
    return dot(matrix, value).astype(BF)


def by_slot(r):
    return (r & 7) * 16 + (r >> 3)


def by_image(r):
    return (r & 15) * 8 + (r >> 4)


def by_expert(r):
    return ((r >> 3) & 7) * 16 + (r >> 6) * 8 + (r & 7)


def by_peer(r):
    return ((r >> 3) & 1) * 64 + (r >> 4) * 8 + (r & 7)


X_FIRST = ((0, 1), (1, 0), (1, 1))


def rows16(index):
    return pl.ds(pl.multiple_of(index * 16, 16), 16)


def kernel(
    tok_h, grad_h, rt_ref, w1_h, w2_h,
    router_out, back_out, disp_out, lg, dw1_h, dw2_h,
    tok, grad, w1, w2, disp, comb, stage, a2a_s, a2a_r, rows, parts, rsb,
    hid, act, act_t, dwk, dws, dwr, fin, back_s, back_r, sb,
    arp, arr, ars, arg, arf,
    s_load, s_w, s_wr, s_a2a, r_a2a, s_ag, r_ag, s_rs, r_rs, s_bk, r_bk,
    s_dw, r_dw, s_dwo, s_ar, r_ar, s_loc,
):
    dp = lax.axis_index("dp")
    ex = lax.axis_index("expert")
    x, zl, core = dp // 4, (dp // 2) % 2, dp % 2
    zh, y = ex // 4, ex % 4

    side = 1 - 2 * core

    def in_dp(dx, dz, dc=0):
        return (((x + 4 + side * dx) % 4) * 4 + ((zl + dz) % 2) * 2 + (core + dc) % 2, ex)

    def ex_of(k, sign=1):
        return ((zh + k // 4) % 2) * 4 + (y + 4 + sign * (k % 4)) % 4

    def peer(k, sign=1):
        flip = (zl + k // 4) % 2
        return (x * 4 + flip * 2 + core, ex_of(k, sign))

    def remote(src, dst, s_sem, r_sem, device):
        return pltpu.make_async_remote_copy(
            src_ref=src, dst_ref=dst, send_sem=s_sem, recv_sem=r_sem,
            device_id=device, device_id_type=MESH,
        )

    barrier = pltpu.get_barrier_semaphore()
    for n in range(1, 16):
        pl.semaphore_signal(
            barrier, inc=1, device_id=in_dp(n // 4, (n // 2) % 2, n % 2), device_id_type=MESH
        )
    for k in range(1, 8):
        pl.semaphore_signal(barrier, inc=1, device_id=peer(k), device_id_type=MESH)

    def load(which, i):
        src, dst = ((tok_h, tok), (grad_h, grad))[which]
        return pltpu.make_async_copy(src.at[i], dst.at[i], s_load.at[which, i])

    for i in range(IMG):
        load(0, i).start()

    rt = rt_ref[...]

    def pre_in(n, carry):
        for u in range(4):
            load(0, 4 * n + u).wait()
            load(1, 4 * n + u).start()
        for u in range(4):
            i = 4 * n + u
            image = tok[i]
            logits = dot_nt(rt, image)
            e1 = jnp.exp(logits - jnp.max(logits, axis=1, keepdims=True))
            d = e1 / jnp.sum(e1, axis=1, keepdims=True)
            e0 = jnp.exp(logits - jnp.max(logits, axis=0, keepdims=True))
            c = e0 / jnp.sum(e0, axis=0, keepdims=True)
            disp[i] = d
            comb[i] = c
            stage[rows16(i)] = dot(d.astype(BF), image).astype(BF)
        return carry

    def pre_grad(n, carry):
        for u in range(4):
            load(1, 4 * n + u).wait()
        for u in range(4):
            i = 4 * n + u
            stage[rows16(i)] = dot(comb[i].astype(BF), grad[i]).astype(BF)
        return carry

    def wait_sent(ref, sem):
        remote(ref, ref, sem, sem, in_dp(1, 0)).wait_send()

    def wait_landed(ref, sem):
        remote(ref, ref, sem, sem, in_dp(1, 0)).wait_recv()

    def start_a2a(a):
        a2a_s[a] = permute_rows(by_slot, stage[...])
        for k in range(1, 8):
            remote(
                a2a_s.at[a, rows16(ex_of(k))], a2a_r.at[a, pl.ds(k * 16, 16)],
                s_a2a.at[a], r_a2a.at[a], peer(k),
            ).start()
        a2a_r[a, pl.ds(0, 16)] = a2a_s[a, rows16(ex)]

    lax.fori_loop(0, IMG // 4, pre_in, 0)
    pl.semaphore_wait(barrier, 22)
    start_a2a(0)
    lax.fori_loop(0, IMG // 4, pre_grad, 0)
    start_a2a(1)

    LAST = ((4, 5, 6, 7), (1, 3, 5, 7))

    def ag_copy(a, j, src_slot, dst_slot, dx, dz):
        sem = 0 if dst_slot in LAST[j] else dst_slot
        remote(
            rows.at[a, j, pl.ds(src_slot * 64, 64)], rows.at[a, j, pl.ds(dst_slot * 64, 64)],
            s_ag.at[a, j], r_ag.at[a, j, sem], in_dp(dx, dz),
        ).start()

    def ag_wait(a, j, slot):
        wait_landed(rows.at[a, j, pl.ds(slot * 64, 64)], r_ag.at[a, j, slot])

    def ag_own(a):
        wait_landed(a2a_r.at[a, pl.ds(16, 112)], r_a2a.at[a])
        ordered = permute_rows(by_expert, a2a_r[a])
        for j in range(2):
            rows[a, j, pl.ds(0, 64)] = ordered[j * 64 : j * 64 + 64]

    def ag_first(a):
        for j in range(2):
            ag_copy(a, j, 0, 2, 1, 0)
            ag_copy(a, j, 0, 1, 0, 1)
            ag_copy(a, j, 0, 6, 3, 0)

    def ag_second(a):
        ag_wait(a, 0, 1)
        ag_copy(a, 0, 1, 3, 1, 0)
        ag_copy(a, 0, 1, 7, 3, 0)
        for j in range(2):
            ag_wait(a, j, 2)
            ag_copy(a, j, 2, 4, 1, 0)
        ag_copy(a, 1, 2, 3, 0, 1)
        ag_wait(a, 1, 6)
        ag_copy(a, 1, 6, 7, 0, 1)

    def ag_third(a):
        ag_wait(a, 0, 3)
        ag_copy(a, 0, 3, 5, 1, 0)
        ag_wait(a, 1, 4)
        ag_copy(a, 1, 4, 5, 0, 1)

    def ag_end(a, j):
        wait_landed(rows.at[a, j, pl.ds(256, 256)], r_ag.at[a, j, 0])

    def project(a, w, j, finish):
        for h in range(2):
            hid[j, pl.ds(h * 256, 256)] = finish(
                j, h, dot_nt(rows[a, j, pl.ds(h * 256, 256)], w[j]))

    def keep(j, h, value):
        return value

    def gelu(j):
        def step(n, carry):
            at = pl.ds(pl.multiple_of(n * 32, 32), 32)
            v = hid[j, at]
            half = 0.5 * (1.0 + lax.erf(v * root_half))
            act[j, at] = (v * half).astype(BF)
            hid[j, at] = half + v * jnp.exp(-0.5 * v * v) * inv_root_tau
            return carry

        lax.fori_loop(0, ROWS // 32, step, 0)

    def slope(j, h, value):
        return value * hid[j, pl.ds(h * 256, 256)]

    def to_parts(o, w, j):
        def step(n, carry):
            at = pl.ds(pl.multiple_of(n * 256, 256), 256)
            parts[o, j, :, at] = dot(act[j], w[j, :, at]).astype(BF)
            return carry

        lax.fori_loop(0, D // 256, step, 0)

    dw = []

    def weight_grad(n, a, j):
        def step(m, carry):
            at = pl.ds(pl.multiple_of(m * 256, 256), 256)
            total = dot(act_t[j], rows[a, j, :, at])
            dwk[n, j, :, at] = total[:HID]
            dws[n, j, :, at] = total[HID:].astype(BF)
            return carry

        lax.fori_loop(0, D // 256, step, 0)
        cp = remote(dws.at[n, j], dwr.at[n, j], s_dw.at[n, j], r_dw.at[n, j], in_dp(0, 0, 1))
        cp.start()
        dw.append((cp, n, j))

    def rs_copy(o, j, first, count, land, sem, dx, dz):
        remote(
            parts.at[o, j, pl.ds(first, count)], rsb.at[o, j, pl.ds(land, count)],
            s_rs.at[o, j], r_rs.at[o, j, sem], in_dp(dx, dz),
        ).start()

    def part(o, j, first, count):
        return parts[o, j, pl.ds(first, count)].astype(F32)

    def landed(o, j, land, count, sem):
        wait_landed(rsb.at[o, j, pl.ds(land, count)], r_rs.at[o, j, sem])
        return rsb[o, j, pl.ds(land, count)].astype(F32)

    def rs_begin(o, j):
        if (o, j) in X_FIRST:
            rs_copy(o, j, 256, 128, 0, 0, 3, 0)
            rs_copy(o, j, 384, 128, 128, 1, 1, 0)
        else:
            for dx in (2, 1, 3, 0):
                rs_copy(o, j, 128 * dx + 64, 64, 64 * dx, 3 + dx, 0, 1)

    def rs_add(o, j, dx):
        total = part(o, j, 128 * dx, 64) + landed(o, j, 64 * dx, 64, 3 + dx)
        parts[o, j, pl.ds(128 * dx, 64)] = total.astype(BF)

    def rs_far(o, j):
        rs_add(o, j, 2)
        rs_copy(o, j, 256, 64, 256, 0, 3, 0)

    def rs_near(o, j):
        rs_add(o, j, 3)
        rs_copy(o, j, 384, 64, 320, 1, 1, 0)
        rs_add(o, j, 1)

    def rs_second(o, j):
        if (o, j) in X_FIRST:
            count, land, last = 128, 0, 256
        else:
            count, land, last = 64, 256, 384
        total = part(o, j, 128, count) + landed(o, j, land, count, 0)
        parts[o, j, pl.ds(128, count)] = total.astype(BF)
        rs_copy(o, j, 128, count, last, 1, 3, 0)

    def rs_third(o, j):
        both = landed(o, j, 128, 256, 1)
        total = part(o, j, 64, 64) + both[64:128] + both[192:256]
        parts[o, j, pl.ds(64, 64)] = total.astype(BF)
        rs_copy(o, j, 64, 64, 384, 2, 0, 1)
        fin[pl.ds(64 * j, 64)] = (part(o, j, 0, 64) + both[:64] + both[128:192])

    def rs_end(o, j):
        if (o, j) in X_FIRST:
            total = fin[pl.ds(64 * j, 64)] + landed(o, j, 384, 64, 2)
        else:
            both = landed(o, j, 320, 128, 1)
            total = part(o, j, 0, 64) + both[:64] + both[64:] + landed(o, j, 0, 64, 3)
        back_s[o, pl.ds(64 * j, 64)] = total.astype(BF)

    def give_back(o):
        back_s[o] = permute_rows(by_peer, back_s[o])
        for k in range(1, 8):
            remote(
                back_s.at[o, pl.ds(k * 16, 16)], back_r.at[o, rows16(ex)],
                s_bk.at[o], r_bk.at[o], peer(k, -1),
            ).start()
        back_r[o, rows16(ex)] = back_s[o, pl.ds(0, 16)]

    def take_back(o):
        wait_landed(back_r.at[o, pl.ds(0, 112)], r_bk.at[o])
        return permute_rows(by_image, back_r[o])

    def hidden_step(j):
        ag_end(0, j)
        project(0, w1, j, keep)
        gelu(j)

    def grad_step(j):
        ag_end(1, j)
        project(1, w2, j, slope)
        act_t[j] = act[j].T
        act[j] = hid[j].astype(BF)
        to_parts(1, w1, j)
        rs_begin(1, j)

    ag_own(0)
    ag_first(0)
    own_w, far_w = [], []
    for n, (src, dst) in enumerate(((w1_h, w1), (w2_h, w2))):
        for j in range(2):
            own_w.append(pltpu.make_async_copy(
                src.at[j], dst.at[j, pl.ds(0, HID)], s_loc.at[n, j]))
            far_w.append(remote(
                src.at[j], dst.at[j, pl.ds(HID, HID)], s_w.at[n, j], s_wr.at[n, j],
                in_dp(0, 0, 1)))
    for cp in own_w + far_w:
        cp.start()
    ag_own(1)
    ag_second(0)
    ag_first(1)
    ag_third(0)
    for cp in own_w:
        cp.wait()
    for cp in far_w:
        cp.wait_recv()
    hidden_step(0)
    ag_second(1)
    to_parts(0, w2, 0)
    rs_begin(0, 0)
    hidden_step(1)
    ag_third(1)
    to_parts(0, w2, 1)
    rs_begin(0, 1)
    grad_step(0)
    rs_second(0, 1)
    grad_step(1)
    rs_far(0, 0)
    rs_near(0, 0)
    weight_grad(1, 1, 0)
    rs_third(0, 1)
    rs_second(1, 0)
    rs_second(0, 0)
    weight_grad(1, 1, 1)
    rs_second(1, 1)
    rs_third(1, 0)
    rs_end(0, 0)
    rs_end(0, 1)
    give_back(0)
    act_t[0] = act[0].T
    weight_grad(0, 0, 0)
    rs_third(1, 1)
    act_t[1] = act[1].T
    weight_grad(0, 0, 1)
    sb[0] = take_back(0)

    def comb_side(n, carry):
        for u in range(4):
            i = 4 * n + u
            g = dot_nt(sb[0, rows16(i)], grad[i])
            c = comb[i]
            comb[i] = c * (g - jnp.sum(c * g, axis=0, keepdims=True))
        return carry

    lax.fori_loop(0, IMG // 4, comb_side, 0)

    rs_end(1, 0)
    rs_end(1, 1)
    give_back(1)

    for cp, n, j in dw:
        cp.wait()
        dws[n, j] = (dwk[n, j] + dwr[n, j].astype(F32)).astype(BF)
        out = (dw1_h, dw2_h)[n]
        pltpu.make_async_copy(dws.at[n, j], out.at[j], s_dwo.at[n, j]).start()

    sb[1] = take_back(1)
    back_out[...] = sb[1]
    for i in range(IMG):
        disp_out[i] = disp[i].astype(BF)

    def disp_side(n, total):
        for u in range(4):
            i = 4 * n + u
            g = dot_nt(sb[1, rows16(i)], tok[i])
            d = disp[i]
            lg[i] = (comb[i] + d * (g - jnp.sum(d * g, axis=1, keepdims=True))).astype(BF)
        for u in range(4):
            i = 4 * n + u
            total = total + dot(lg[i], tok[i])
        return total

    term = lax.fori_loop(0, IMG // 4, disp_side, jnp.zeros((S, D), F32))
    for p in range(8):
        lane = 384 * (p // 2)
        width = min(384, D - lane)
        arp[p, :, pl.ds(0, width)] = term[8 * (p % 2) : 8 * (p % 2) + 8, lane : lane + width]
        if width < 384:
            arp[p, :, pl.ds(width, 384 - width)] = jnp.zeros((8, 384 - width), F32)

    for k in range(1, 8):
        remote(arp.at[ex_of(k)], arr.at[k], s_ar.at[0], r_ar.at[0], peer(k)).start()
    for n in range(2):
        wait_sent(a2a_s.at[n, pl.ds(0, 112)], s_a2a.at[n])
        wait_sent(back_s.at[n, pl.ds(0, 112)], s_bk.at[n])
        for j in range(2):
            wait_sent(rows.at[n, j, pl.ds(64, 448)], s_ag.at[n, j])
            wait_sent(rsb.at[n, j], s_rs.at[n, j])
    wait_landed(arr.at[pl.ds(1, 7)], r_ar.at[0])
    total = arp[ex]
    for k in range(1, 8):
        total = total + arr[k]
    ars[0] = total
    for n in range(1, 16):
        remote(
            ars.at[0], arg.at[dp], s_ar.at[1], r_ar.at[1], in_dp(n // 4, (n // 2) % 2, n % 2)
        ).start()
    arg[dp] = total
    for cp in far_w:
        cp.wait_send()
    for n in range(2):
        for j in range(2):
            out = (dw1_h, dw2_h)[n]
            pltpu.make_async_copy(dws.at[n, j], out.at[j], s_dwo.at[n, j]).wait()
    wait_landed(arg.at[pl.ds(0, 15)], r_ar.at[1])
    total = arg[0]
    for n in range(1, 16):
        total = total + arg[n]
    ars[1] = total
    for k in range(1, 8):
        remote(ars.at[1], arf.at[ex], s_ar.at[2], r_ar.at[2], peer(k)).start()
    arf[ex] = total
    wait_sent(arp.at[pl.ds(0, 7)], s_ar.at[0])
    wait_sent(arg.at[pl.ds(0, 15)], s_ar.at[1])
    wait_landed(arf.at[pl.ds(0, 7)], r_ar.at[2])
    for p in range(8):
        lane = 384 * (p // 2)
        width = min(384, D - lane)
        router_out[pl.ds(8 * (p % 2), 8), pl.ds(lane, width)] = arf[p, :, pl.ds(0, width)]
    wait_sent(arf.at[pl.ds(0, 7)], s_ar.at[2])


def token_kernel(
    rt_ref, router_ref, back_ref, disp_ref, lg_ref, dw1_in, dw2_in,
    token_grad_h, router_out, dw1_h, dw2_h, tgo, dwv, s_out, s_in, s_dw,
):
    reads, writes = [], []
    for n, (src, dst) in enumerate(((dw1_in, dw1_h), (dw2_in, dw2_h))):
        reads.append(pltpu.make_async_copy(src, dwv.at[n], s_in.at[n]))
        writes.append(pltpu.make_async_copy(dwv.at[n], dst, s_dw.at[n]))
    for cp in reads:
        cp.start()
    router_out[...] = router_ref[...]
    for i in range(IMG):
        left = jnp.concatenate([disp_ref[i], lg_ref[i]], axis=0)
        right = jnp.concatenate([back_ref[pl.ds(i * 16, 16)], rt_ref[...]], axis=0)
        tgo[i] = dot_tn(left, right).astype(BF)
        cp = pltpu.make_async_copy(tgo.at[i], token_grad_h.at[i], s_out.at[i])
        cp.start()
        writes.append(cp)
        if i in (2, 4):
            reads[i // 2 - 1].wait()
            writes[i // 2 - 1].start()
    for cp in writes:
        cp.wait()


def shards(tokens, router, weight_in, weight_out, out_grad):
    any_space = pl.BlockSpec(memory_space=pl.ANY)
    vmem = pl.BlockSpec(memory_space=pltpu.VMEM)
    dma = pltpu.SemaphoreType.DMA
    V = pltpu.VMEM
    router_t = router.T
    router_grad, back, disp_half, grad_logit, dw1, dw2 = pl.pallas_call(
        kernel,
        name="soft_moe",
        out_shape=(
            jax.ShapeDtypeStruct((S, D), F32),
            jax.ShapeDtypeStruct((128, D), BF),
            jax.ShapeDtypeStruct((IMG, S, M), BF),
            jax.ShapeDtypeStruct((IMG, S, M), BF),
            jax.ShapeDtypeStruct((2, HID, D), BF),
            jax.ShapeDtypeStruct((2, HID, D), BF),
        ),
        in_specs=[any_space, any_space, vmem, any_space, any_space],
        out_specs=(vmem, vmem, vmem, vmem, any_space, any_space),
        scratch_shapes=[
            V((IMG, M, D), BF), V((IMG, M, D), BF),
            V((2, HID2, D), BF), V((2, HID2, D), BF),
            V((IMG, S, M), F32), V((IMG, S, M), F32),
            V((128, D), BF), V((2, 128, D), BF), V((2, 128, D), BF),
            V((2, 2, ROWS, D), BF), V((2, 2, ROWS, D), BF),
            V((2, 2, 448, D), BF),
            V((2, ROWS, HID2), F32), V((2, ROWS, HID2), BF), V((2, HID2, ROWS), BF),
            V((2, 2, HID, D), F32), V((2, 2, HID, D), BF), V((2, 2, HID, D), BF),
            V((128, D), F32), V((2, 128, D), BF), V((2, 128, D), BF),
            V((2, 128, D), BF),
            V((8, 8, 384), F32), V((8, 8, 384), F32), V((2, 8, 384), F32),
            V((16, 8, 384), F32), V((8, 8, 384), F32),
            dma((2, IMG)), dma((2, 2)), dma((2, 2)), dma((2,)), dma((2,)),
            dma((2, 2)), dma((2, 2, 8)), dma((2, 2)), dma((2, 2, 8)),
            dma((2,)), dma((2,)), dma((2, 2)), dma((2, 2)), dma((2, 2)),
            dma((3,)), dma((3,)), dma((2, 2)),
        ],
        compiler_params=pltpu.CompilerParams(
            collective_id=0, has_side_effects=True, vmem_limit_bytes=62 * 2**20
        ),
    )(tokens, out_grad, router_t, jnp.swapaxes(weight_in, 1, 2), weight_out)
    token_grad, router_grad, dw1, dw2 = pl.pallas_call(
        token_kernel,
        name="token_grad",
        out_shape=(
            jax.ShapeDtypeStruct((IMG, M, D), BF),
            jax.ShapeDtypeStruct((S, D), F32),
            jax.ShapeDtypeStruct((2, HID, D), BF),
            jax.ShapeDtypeStruct((2, HID, D), BF),
        ),
        in_specs=[vmem] * 5 + [any_space] * 2,
        out_specs=(any_space, vmem, any_space, any_space),
        scratch_shapes=[
            V((IMG, M, D), BF), V((2, 2, HID, D), BF), dma((IMG,)), dma((2,)), dma((2,)),
        ],
        compiler_params=pltpu.CompilerParams(vmem_limit_bytes=62 * 2**20),
    )(router_t, router_grad, back, disp_half, grad_logit, dw1, dw2)
    return token_grad, router_grad.T, jnp.swapaxes(dw1, 1, 2), dw2


def solution(mesh):
    in_specs = (
        P(("dp", "expert"), None, None),
        P(),
        P("expert", None, "dp"),
        P("expert", "dp", None),
        P(("dp", "expert"), None, None),
    )
    out_specs = (
        P(("dp", "expert"), None, None),
        P(),
        P("expert", None, "dp"),
        P("expert", "dp", None),
    )
    return jax.shard_map(shards, mesh=mesh, in_specs=in_specs, out_specs=out_specs, check_vma=False)
```

```python
import jax
import jax.numpy as jnp
from jax import lax
from jax.experimental import pallas as pl
from jax.experimental.pallas import tpu as pltpu
from jax.sharding import PartitionSpec as P

MESH = pl.DeviceIdType.MESH
BF = jnp.bfloat16
F32 = jnp.float32

D = 1280
M = 256
S = 16
IMG = 8
HID = 320
HID2 = 640
ROWS = 512

root_half = 0.7071067811865476
inv_root_tau = 0.3989422804014327

NT = (((1,), (1,)), ((), ()))
TN = (((0,), (0,)), ((), ()))


def dot(a, b):
    return jnp.dot(a, b, preferred_element_type=F32)


def dot_nt(a, b):
    return lax.dot_general(a, b, NT, preferred_element_type=F32)


def dot_tn(a, b):
    return lax.dot_general(a, b, TN, preferred_element_type=F32)


def permute_rows(source_of, value):
    r = lax.broadcasted_iota(jnp.int32, (128, 128), 0)
    c = lax.broadcasted_iota(jnp.int32, (128, 128), 1)
    matrix = jnp.where(c == source_of(r), 1.0, 0.0).astype(BF)
    return dot(matrix, value).astype(BF)


def by_slot(r):
    return (r & 7) * 16 + (r >> 3)


def by_image(r):
    return (r & 15) * 8 + (r >> 4)


def by_expert(r):
    return ((r >> 3) & 7) * 16 + (r >> 6) * 8 + (r & 7)


def by_peer(r):
    return ((r >> 3) & 1) * 64 + (r >> 4) * 8 + (r & 7)


WHOLE, TOP, BOTTOM = (0, 64), (0, 32), (32, 32)
PIECES = (
    (((WHOLE, False),), ((WHOLE, True),)),
    (((TOP, False), (BOTTOM, True)), ((WHOLE, True),)),
)


def rows16(index):
    return pl.ds(pl.multiple_of(index * 16, 16), 16)


def kernel(
    tok_h, grad_h, rt_h, w1_h, w2_h,
    router_out, back_h, disp_h, lg_h, dw1_h, dw2_h,
    tok, grad, w1, w2, disp, comb, stage, a2a_s, a2a_r, rows, parts, rsb,
    hid, act, act_t, dwk, dws, dwr, back_s, back_r, sb,
    arp, arr, ars, arg, arf, rt_v, disp_b, lg,
    s_load, s_w, s_wr, s_a2a, r_a2a, s_ag, r_ag, s_rs, r_rs, s_bk, r_bk,
    s_dw, r_dw, s_dwo, s_ar, r_ar, s_loc, s_rt,
):
    dp = lax.axis_index("dp")
    ex = lax.axis_index("expert")
    x, zl, core = dp // 4, (dp // 2) % 2, dp % 2
    zh, y = ex // 4, ex % 4

    side = 1 - 2 * core

    def in_dp(dx, dz, dc=0):
        return (((x + 4 + side * dx) % 4) * 4 + ((zl + dz) % 2) * 2 + (core + dc) % 2, ex)

    def ex_of(k, sign=1):
        return ((zh + k // 4) % 2) * 4 + (y + 4 + sign * (k % 4)) % 4

    def peer(k, sign=1):
        flip = (zl + k // 4) % 2
        return (x * 4 + flip * 2 + core, ex_of(k, sign))

    def remote(src, dst, s_sem, r_sem, device):
        return pltpu.make_async_remote_copy(
            src_ref=src, dst_ref=dst, send_sem=s_sem, recv_sem=r_sem,
            device_id=device, device_id_type=MESH,
        )

    def load(which, i):
        src, dst = ((tok_h, tok), (grad_h, grad))[which]
        return pltpu.make_async_copy(src.at[i], dst.at[i], s_load.at[which, i])

    load_rt = pltpu.make_async_copy(rt_h, rt_v, s_rt.at[0])
    load_rt.start()
    for i in range(IMG):
        load(0, i).start()

    barrier = pltpu.get_barrier_semaphore()
    for n in range(1, 16):
        pl.semaphore_signal(
            barrier, inc=1, device_id=in_dp(n // 4, (n // 2) % 2, n % 2), device_id_type=MESH
        )
    for k in range(1, 8):
        pl.semaphore_signal(barrier, inc=1, device_id=peer(k), device_id_type=MESH)

    load_rt.wait()
    rt = rt_v[...]

    def pre_in(n, carry):
        for u in range(4):
            load(0, 4 * n + u).wait()
            load(1, 4 * n + u).start()
        for u in range(4):
            i = 4 * n + u
            image = tok[i]
            logits = dot_nt(rt, image)
            e1 = jnp.exp(logits - jnp.max(logits, axis=1, keepdims=True))
            d = e1 / jnp.sum(e1, axis=1, keepdims=True)
            e0 = jnp.exp(logits - jnp.max(logits, axis=0, keepdims=True))
            c = e0 / jnp.sum(e0, axis=0, keepdims=True)
            disp[i] = d
            disp_b[i] = d.astype(BF)
            comb[i] = c
            stage[rows16(i)] = dot(d.astype(BF), image).astype(BF)
        return carry

    def pre_grad(n, carry):
        for u in range(4):
            load(1, 4 * n + u).wait()
        for u in range(4):
            i = 4 * n + u
            stage[rows16(i)] = dot(comb[i].astype(BF), grad[i]).astype(BF)
        return carry

    def wait_sent(ref, sem):
        remote(ref, ref, sem, sem, in_dp(1, 0)).wait_send()

    def wait_landed(ref, sem):
        remote(ref, ref, sem, sem, in_dp(1, 0)).wait_recv()

    def start_a2a(a):
        a2a_s[a] = permute_rows(by_slot, stage[...])
        for k in range(1, 8):
            remote(
                a2a_s.at[a, rows16(ex_of(k))], a2a_r.at[a, pl.ds(k * 16, 16)],
                s_a2a.at[a], r_a2a.at[a], peer(k),
            ).start()
        a2a_r[a, pl.ds(0, 16)] = a2a_s[a, rows16(ex)]

    lax.fori_loop(0, IMG // 4, pre_in, 0)
    pl.semaphore_wait(barrier, 22)
    start_a2a(0)
    lax.fori_loop(0, IMG // 4, pre_grad, 0)
    start_a2a(1)

    LAST = ((4, 5, 6, 7), (1, 3, 5, 7))

    def ag_copy(a, j, src_slot, dst_slot, dx, dz):
        sem = 0 if dst_slot in LAST[j] else dst_slot
        remote(
            rows.at[a, j, pl.ds(src_slot * 64, 64)], rows.at[a, j, pl.ds(dst_slot * 64, 64)],
            s_ag.at[a, j], r_ag.at[a, j, sem], in_dp(dx, dz),
        ).start()

    def ag_wait(a, j, slot):
        wait_landed(rows.at[a, j, pl.ds(slot * 64, 64)], r_ag.at[a, j, slot])

    def ag_own(a):
        wait_landed(a2a_r.at[a, pl.ds(16, 112)], r_a2a.at[a])
        ordered = permute_rows(by_expert, a2a_r[a])
        for j in range(2):
            rows[a, j, pl.ds(0, 64)] = ordered[j * 64 : j * 64 + 64]

    def ag_first(a):
        for j in range(2):
            ag_copy(a, j, 0, 2, 1, 0)
            ag_copy(a, j, 0, 1, 0, 1)
            ag_copy(a, j, 0, 6, 3, 0)

    def ag_second(a):
        ag_wait(a, 0, 1)
        ag_copy(a, 0, 1, 3, 1, 0)
        ag_copy(a, 0, 1, 7, 3, 0)
        for j in range(2):
            ag_wait(a, j, 2)
            ag_copy(a, j, 2, 4, 1, 0)
        ag_copy(a, 1, 2, 3, 0, 1)
        ag_wait(a, 1, 6)
        ag_copy(a, 1, 6, 7, 0, 1)

    def ag_third(a):
        ag_wait(a, 0, 3)
        ag_copy(a, 0, 3, 5, 1, 0)
        ag_wait(a, 1, 4)
        ag_copy(a, 1, 4, 5, 0, 1)

    def ag_end(a, j):
        wait_landed(rows.at[a, j, pl.ds(256, 256)], r_ag.at[a, j, 0])

    def project(a, w, j, finish):
        for h in range(2):
            hid[j, pl.ds(h * 256, 256)] = finish(
                j, h, dot_nt(rows[a, j, pl.ds(h * 256, 256)], w[j]))

    def keep(j, h, value):
        return value

    def gelu(j):
        def step(n, carry):
            at = pl.ds(pl.multiple_of(n * 32, 32), 32)
            v = hid[j, at]
            half = 0.5 * (1.0 + lax.erf(v * root_half))
            act[j, at] = (v * half).astype(BF)
            hid[j, at] = half + v * jnp.exp(-0.5 * v * v) * inv_root_tau
            return carry

        lax.fori_loop(0, ROWS // 32, step, 0)

    def slope(j, h, value):
        return value * hid[j, pl.ds(h * 256, 256)]

    def to_parts(o, w, j):
        def step(n, carry):
            at = pl.ds(pl.multiple_of(n * 256, 256), 256)
            total = dot(act[j], w[j, :, at]).astype(BF)
            parts[o, j, :, :, at] = total.reshape(8, 64, 256)
            return carry

        lax.fori_loop(0, D // 256, step, 0)

    dw = []

    def weight_grad(n, a, j):
        def step(m, carry):
            at = pl.ds(pl.multiple_of(m * 256, 256), 256)
            total = dot(act_t[j], rows[a, j, :, at])
            dwk[n, j, :, at] = total[:HID]
            dws[n, j, :, at] = total[HID:].astype(BF)
            return carry

        lax.fori_loop(0, D // 256, step, 0)
        cp = remote(dws.at[n, j], dwr.at[n, j], s_dw.at[n, j], r_dw.at[n, j], in_dp(0, 0, 1))
        cp.start()
        dw.append((cp, n, j))

    FAR, NEAR = (3, 0), (4, 1)

    def rs_copy(o, j, piece, slot, count, land, sem, dx, dz):
        at = pl.ds(*piece)
        remote(
            parts.at[o, j, pl.ds(slot, count), at], rsb.at[o, j, pl.ds(land, count), at],
            s_rs.at[o, j], r_rs.at[o, j, sem + 8 * (piece[0] // 32)], in_dp(dx, dz),
        ).start()

    def part(o, j, piece, slot, count=1):
        return parts[o, j, pl.ds(slot, count), pl.ds(*piece)].astype(F32)

    def landed(o, j, piece, land, count, sem):
        ref = rsb.at[o, j, pl.ds(land, count), pl.ds(*piece)]
        wait_landed(ref, r_rs.at[o, j, sem + 8 * (piece[0] // 32)])
        return ref[...].astype(F32)

    def rs_begin(o, j):
        for piece, x_first in PIECES[o][j]:
            if x_first:
                for dz in (1, 0):
                    rs_copy(o, j, piece, 4 + dz, 1, dz, FAR[dz], 3, 0)
                for dz in (1, 0):
                    rs_copy(o, j, piece, 6 + dz, 1, 2 + dz, NEAR[dz], 1, 0)
            else:
                for dx in (2, 3, 1, 0):
                    rs_copy(o, j, piece, 2 * dx + 1, 1, dx, 3 + dx, 0, 1)

    def rs_add(o, j, piece, dx):
        total = part(o, j, piece, 2 * dx) + landed(o, j, piece, dx, 1, 3 + dx)
        parts[o, j, pl.ds(2 * dx, 1), pl.ds(*piece)] = total.astype(BF)

    def rs_far(o, j, piece):
        rs_add(o, j, piece, 2)
        rs_copy(o, j, piece, 4, 1, 4, 0, 3, 0)

    def rs_near(o, j, piece):
        rs_add(o, j, piece, 3)
        rs_copy(o, j, piece, 6, 1, 5, 1, 1, 0)
        rs_add(o, j, piece, 1)

    def rs_second(o, j, which=0):
        piece, x_first = PIECES[o][j][which]
        for slot, land, sem, last, last_sem in (
            ((3, 1, FAR[1], 5, NEAR[1]), (2, 0, FAR[0], 4, NEAR[0])) if x_first
            else ((2, 4, 0, 6, 1),)
        ):
            total = part(o, j, piece, slot) + landed(o, j, piece, land, 1, sem)
            parts[o, j, pl.ds(slot, 1), pl.ds(*piece)] = total.astype(BF)
            rs_copy(o, j, piece, slot, 1, last, last_sem, 3, 0)

    def ring_total(o, j, piece, dz):
        at = pl.ds(*piece)
        wait_landed(rsb.at[o, j, pl.ds(2, 2), at], r_rs.at[o, j, NEAR[dz] + 8 * (piece[0] // 32)])
        right, left = rsb[o, j, 2 + dz, at], rsb[o, j, 4 + dz, at]
        return part(o, j, piece, dz)[0] + right.astype(F32) + left.astype(F32)

    def rs_third(o, j, which=0):
        piece = PIECES[o][j][which][0]
        parts[o, j, 1, pl.ds(*piece)] = ring_total(o, j, piece, 1).astype(BF)
        rs_copy(o, j, piece, 1, 1, 6, 2, 0, 1)

    def rs_end(o, j):
        for piece, x_first in PIECES[o][j]:
            if x_first:
                total = ring_total(o, j, piece, 0) + landed(o, j, piece, 6, 1, 2)[0]
            else:
                both = landed(o, j, piece, 5, 2, 1)
                total = part(o, j, piece, 0)[0] + both[0] + both[1] + landed(o, j, piece, 0, 1, 3)[0]
            back_s[o, pl.ds(64 * j + piece[0], piece[1])] = total.astype(BF)

    def give_back(o):
        back_s[o] = permute_rows(by_peer, back_s[o])
        for k in range(1, 8):
            remote(
                back_s.at[o, pl.ds(k * 16, 16)], back_r.at[o, rows16(ex)],
                s_bk.at[o], r_bk.at[o], peer(k, -1),
            ).start()
        back_r[o, rows16(ex)] = back_s[o, pl.ds(0, 16)]

    def take_back(o):
        wait_landed(back_r.at[o, pl.ds(0, 112)], r_bk.at[o])
        return permute_rows(by_image, back_r[o])

    def hidden_step(j):
        ag_end(0, j)
        project(0, w1, j, keep)
        gelu(j)

    def grad_step(j):
        ag_end(1, j)
        project(1, w2, j, slope)
        act_t[j] = act[j].T
        act[j] = hid[j].astype(BF)
        to_parts(1, w1, j)
        rs_begin(1, j)

    ag_own(0)
    ag_first(0)
    own_w, far_w = [], []
    for n, (src, dst) in enumerate(((w1_h, w1), (w2_h, w2))):
        for j in range(2):
            own_w.append(pltpu.make_async_copy(
                src.at[j], dst.at[j, pl.ds(0, HID)], s_loc.at[n, j]))
            far_w.append(remote(
                src.at[j], dst.at[j, pl.ds(HID, HID)], s_w.at[n, j], s_wr.at[n, j],
                in_dp(0, 0, 1)))
    for cp in own_w + far_w:
        cp.start()
    ag_own(1)
    ag_second(0)
    ag_first(1)
    ag_third(0)
    for cp in own_w:
        cp.wait()
    for cp in far_w:
        cp.wait_recv()
    ag_second(1)
    hidden_step(0)
    to_parts(0, w2, 0)
    rs_begin(0, 0)
    hidden_step(1)
    ag_third(1)
    to_parts(0, w2, 1)
    rs_begin(0, 1)
    grad_step(0)
    rs_second(0, 1)
    grad_step(1)
    weight_grad(1, 1, 0)
    weight_grad(1, 1, 1)
    act_t[0] = act[0].T
    weight_grad(0, 0, 0)
    rs_second(1, 0, 1)
    rs_far(0, 0, WHOLE)
    rs_near(0, 0, WHOLE)
    rs_third(0, 1)
    rs_second(1, 1)
    rs_second(0, 0)
    rs_far(1, 0, TOP)
    act_t[1] = act[1].T
    weight_grad(0, 0, 1)
    rs_near(1, 0, TOP)
    rs_third(1, 0, 1)
    rs_second(1, 0, 0)
    rs_end(0, 1)
    rs_third(1, 1)
    rs_end(0, 0)
    give_back(0)
    rs_end(1, 0)
    rs_end(1, 1)
    give_back(1)
    sb[0] = take_back(0)

    def comb_side(n, carry):
        for u in range(4):
            i = 4 * n + u
            g = dot_nt(sb[0, rows16(i)], grad[i])
            c = comb[i]
            comb[i] = c * (g - jnp.sum(c * g, axis=0, keepdims=True))
        return carry

    lax.fori_loop(0, IMG // 4, comb_side, 0)

    sb[1] = take_back(1)
    small = [
        pltpu.make_async_copy(sb.at[1], back_h, s_rt.at[0]),
        pltpu.make_async_copy(disp_b, disp_h, s_rt.at[1]),
        pltpu.make_async_copy(lg, lg_h, s_rt.at[2]),
    ]

    def disp_side(n, total):
        for u in range(4):
            i = 4 * n + u
            g = dot_nt(sb[1, rows16(i)], tok[i])
            d = disp[i]
            lg[i] = (comb[i] + d * (g - jnp.sum(d * g, axis=1, keepdims=True))).astype(BF)
        for u in range(4):
            i = 4 * n + u
            total = total + dot(lg[i], tok[i])
        return total

    term = lax.fori_loop(0, IMG // 4, disp_side, jnp.zeros((S, D), F32))
    for p in range(8):
        lane = 384 * (p // 2)
        width = min(384, D - lane)
        arp[p, :, pl.ds(0, width)] = term[8 * (p % 2) : 8 * (p % 2) + 8, lane : lane + width]
        if width < 384:
            arp[p, :, pl.ds(width, 384 - width)] = jnp.zeros((8, 384 - width), F32)

    for k in range(1, 8):
        remote(arp.at[ex_of(k)], arr.at[k], s_ar.at[0], r_ar.at[0], peer(k)).start()
    for cp in small:
        cp.start()
    for n in range(2):
        wait_sent(a2a_s.at[n, pl.ds(0, 112)], s_a2a.at[n])
        wait_sent(back_s.at[n, pl.ds(0, 112)], s_bk.at[n])
        for j in range(2):
            wait_sent(rows.at[n, j, pl.ds(64, 448)], s_ag.at[n, j])
            wait_sent(rsb.at[n, j], s_rs.at[n, j])
    wait_landed(arr.at[pl.ds(1, 7)], r_ar.at[0])
    total = arp[ex]
    for k in range(1, 8):
        total = total + arr[k]
    ars[0] = total
    for n in range(1, 16):
        remote(
            ars.at[0], arg.at[dp], s_ar.at[1], r_ar.at[1], in_dp(n // 4, (n // 2) % 2, n % 2)
        ).start()
    arg[dp] = total
    for cp in far_w:
        cp.wait_send()

    for cp, n, j in dw:
        cp.wait()
        dws[n, j] = (dwk[n, j] + dwr[n, j].astype(F32)).astype(BF)
        out = (dw1_h, dw2_h)[n]
        pltpu.make_async_copy(dws.at[n, j], out.at[j], s_dwo.at[n, j]).start()

    wait_landed(arg.at[pl.ds(0, 15)], r_ar.at[1])
    total = arg[0]
    for n in range(1, 16):
        total = total + arg[n]
    ars[1] = total
    for k in range(1, 8):
        remote(ars.at[1], arf.at[ex], s_ar.at[2], r_ar.at[2], peer(k)).start()
    arf[ex] = total
    wait_sent(arp.at[pl.ds(0, 7)], s_ar.at[0])
    wait_sent(arg.at[pl.ds(0, 15)], s_ar.at[1])
    for cp in small:
        cp.wait()
    for n in range(2):
        for j in range(2):
            out = (dw1_h, dw2_h)[n]
            pltpu.make_async_copy(dws.at[n, j], out.at[j], s_dwo.at[n, j]).wait()
    wait_landed(arf.at[pl.ds(0, 7)], r_ar.at[2])
    for p in range(8):
        lane = 384 * (p // 2)
        width = min(384, D - lane)
        router_out[pl.ds(8 * (p % 2), 8), pl.ds(lane, width)] = arf[p, :, pl.ds(0, width)]
    wait_sent(arf.at[pl.ds(0, 7)], s_ar.at[2])


def token_kernel(
    rt_h, router_h, back_h, disp_h, lg_h, dw1_in, dw2_in,
    token_grad_h, router_out, dw1_h, dw2_h,
    rt_v, router_v, back_v, disp_v, lg_v, tgo, dwv, s_small, s_out, s_in, s_dw,
):
    small = [
        pltpu.make_async_copy(src, dst, s_small.at[n])
        for n, (src, dst) in enumerate((
            (rt_h, rt_v), (back_h, back_v), (disp_h, disp_v), (lg_h, lg_v), (router_h, router_v)))
    ]
    reads, writes = [], []
    for n, (src, dst) in enumerate(((dw1_in, dw1_h), (dw2_in, dw2_h))):
        reads.append(pltpu.make_async_copy(src, dwv.at[n], s_in.at[n]))
        writes.append(pltpu.make_async_copy(dwv.at[n], dst, s_dw.at[n]))
    router_write = pltpu.make_async_copy(router_v, router_out, s_small.at[5])
    for cp in small + reads:
        cp.start()
    for cp in small:
        cp.wait()
    router_write.start()
    for i in range(IMG):
        left = jnp.concatenate([disp_v[i], lg_v[i]], axis=0)
        right = jnp.concatenate([back_v[pl.ds(i * 16, 16)], rt_v[...]], axis=0)
        tgo[i] = dot_tn(left, right).astype(BF)
        cp = pltpu.make_async_copy(tgo.at[i], token_grad_h.at[i], s_out.at[i])
        cp.start()
        writes.append(cp)
        if i in (1, 3):
            reads[i // 2].wait()
            writes[i // 2].start()
    for cp in writes + [router_write]:
        cp.wait()


def shards(tokens, router, weight_in, weight_out, out_grad):
    any_space = pl.BlockSpec(memory_space=pl.ANY)
    vmem = pl.BlockSpec(memory_space=pltpu.VMEM)
    dma = pltpu.SemaphoreType.DMA
    V = pltpu.VMEM
    router_t = router.T
    router_grad, back, disp_half, grad_logit, dw1, dw2 = pl.pallas_call(
        kernel,
        name="soft_moe",
        out_shape=(
            jax.ShapeDtypeStruct((S, D), F32),
            jax.ShapeDtypeStruct((128, D), BF),
            jax.ShapeDtypeStruct((IMG, S, M), BF),
            jax.ShapeDtypeStruct((IMG, S, M), BF),
            jax.ShapeDtypeStruct((2, HID, D), BF),
            jax.ShapeDtypeStruct((2, HID, D), BF),
        ),
        in_specs=[any_space] * 5,
        out_specs=(vmem,) + (any_space,) * 5,
        scratch_shapes=[
            V((IMG, M, D), BF), V((IMG, M, D), BF),
            V((2, HID2, D), BF), V((2, HID2, D), BF),
            V((IMG, S, M), F32), V((IMG, S, M), F32),
            V((128, D), BF), V((2, 128, D), BF), V((2, 128, D), BF),
            V((2, 2, ROWS, D), BF), V((2, 2, 8, 64, D), BF),
            V((2, 2, 7, 64, D), BF),
            V((2, ROWS, HID2), F32), V((2, ROWS, HID2), BF), V((2, HID2, ROWS), BF),
            V((2, 2, HID, D), F32), V((2, 2, HID, D), BF), V((2, 2, HID, D), BF),
            V((2, 128, D), BF), V((2, 128, D), BF),
            V((2, 128, D), BF),
            V((8, 8, 384), F32), V((8, 8, 384), F32), V((2, 8, 384), F32),
            V((16, 8, 384), F32), V((8, 8, 384), F32),
            V((S, D), BF), V((IMG, S, M), BF), V((IMG, S, M), BF),
            dma((2, IMG)), dma((2, 2)), dma((2, 2)), dma((2,)), dma((2,)),
            dma((2, 2)), dma((2, 2, 8)), dma((2, 2)), dma((2, 2, 16)),
            dma((2,)), dma((2,)), dma((2, 2)), dma((2, 2)), dma((2, 2)),
            dma((3,)), dma((3,)), dma((2, 2)), dma((3,)),
        ],
        compiler_params=pltpu.CompilerParams(
            collective_id=0, has_side_effects=True, vmem_limit_bytes=62 * 2**20
        ),
    )(tokens, out_grad, router_t, jnp.swapaxes(weight_in, 1, 2), weight_out)
    token_grad, router_grad, dw1, dw2 = pl.pallas_call(
        token_kernel,
        name="token_grad",
        out_shape=(
            jax.ShapeDtypeStruct((IMG, M, D), BF),
            jax.ShapeDtypeStruct((S, D), F32),
            jax.ShapeDtypeStruct((2, HID, D), BF),
            jax.ShapeDtypeStruct((2, HID, D), BF),
        ),
        in_specs=[any_space] * 7,
        out_specs=(any_space,) * 4,
        scratch_shapes=[
            V((S, D), BF), V((S, D), F32), V((128, D), BF), V((IMG, S, M), BF), V((IMG, S, M), BF),
            V((IMG, M, D), BF), V((2, 2, HID, D), BF), dma((6,)), dma((IMG,)), dma((2,)), dma((2,)),
        ],
        compiler_params=pltpu.CompilerParams(vmem_limit_bytes=62 * 2**20),
    )(router_t, router_grad, back, disp_half, grad_logit, dw1, dw2)
    return token_grad, router_grad.T, jnp.swapaxes(dw1, 1, 2), dw2


def solution(mesh):
    in_specs = (
        P(("dp", "expert"), None, None),
        P(),
        P("expert", None, "dp"),
        P("expert", "dp", None),
        P(("dp", "expert"), None, None),
    )
    out_specs = (
        P(("dp", "expert"), None, None),
        P(),
        P("expert", None, "dp"),
        P("expert", "dp", None),
    )
    return jax.shard_map(shards, mesh=mesh, in_specs=in_specs, out_specs=out_specs, check_vma=False)
```

```python
import jax
import jax.numpy as jnp
from jax import lax
from jax.experimental import pallas as pl
from jax.experimental.pallas import tpu as pltpu
from jax.sharding import PartitionSpec as P

MESH = pl.DeviceIdType.MESH
BF = jnp.bfloat16
F32 = jnp.float32

D = 1280
M = 256
S = 16
IMG = 8
HID = 320
HID2 = 640
ROWS = 512

root_half = 0.7071067811865476
inv_root_tau = 0.3989422804014327

NT = (((1,), (1,)), ((), ()))
TN = (((0,), (0,)), ((), ()))


def dot(a, b):
    return jnp.dot(a, b, preferred_element_type=F32)


def dot_nt(a, b):
    return lax.dot_general(a, b, NT, preferred_element_type=F32)


def dot_tn(a, b):
    return lax.dot_general(a, b, TN, preferred_element_type=F32)


def permute_rows(source_of, value):
    r = lax.broadcasted_iota(jnp.int32, (128, 128), 0)
    c = lax.broadcasted_iota(jnp.int32, (128, 128), 1)
    matrix = jnp.where(c == source_of(r), 1.0, 0.0).astype(BF)
    return dot(matrix, value).astype(BF)


def by_slot(r):
    return (r & 7) * 16 + (r >> 3)


def by_image(r):
    return (r & 15) * 8 + (r >> 4)


def by_expert(r):
    return ((r >> 3) & 7) * 16 + (r >> 6) * 8 + (r & 7)


def by_peer(r):
    return ((r >> 3) & 1) * 64 + (r >> 4) * 8 + (r & 7)


WHOLE, TOP, BOTTOM = (0, 64), (0, 32), (32, 32)
PIECES = (
    (((WHOLE, False),), ((WHOLE, True),)),
    (((TOP, False), (BOTTOM, True)), ((WHOLE, True),)),
)


def rows16(index):
    return pl.ds(pl.multiple_of(index * 16, 16), 16)


def kernel(
    tok_h, grad_h, rt_h, w1_h, w2_h,
    router_out, back_h, disp_h, lg_h, dw1_h, dw2_h,
    tok, grad, w1, w2, disp, comb, stage, a2a_s, a2a_r, rows, parts, rsb,
    hid, act, act_t, dwk, dws, dwr, back_s, back_r, sb,
    arp, arr, ars, arg, arf, rt_v, disp_b, lg,
    s_load, s_w, s_wr, s_a2a, r_a2a, s_ag, r_ag, s_rs, r_rs, s_bk, r_bk,
    s_dw, r_dw, s_dwo, s_ar, r_ar, s_loc, s_rt,
):
    dp = lax.axis_index("dp")
    ex = lax.axis_index("expert")
    x, zl, core = dp // 4, (dp // 2) % 2, dp % 2
    zh, y = ex // 4, ex % 4

    side = 1 - 2 * core

    def in_dp(dx, dz, dc=0):
        return (((x + 4 + side * dx) % 4) * 4 + ((zl + dz) % 2) * 2 + (core + dc) % 2, ex)

    def ex_of(k, sign=1):
        return ((zh + k // 4) % 2) * 4 + (y + 4 + sign * (k % 4)) % 4

    def peer(k, sign=1):
        flip = (zl + k // 4) % 2
        return (x * 4 + flip * 2 + core, ex_of(k, sign))

    def remote(src, dst, s_sem, r_sem, device):
        return pltpu.make_async_remote_copy(
            src_ref=src, dst_ref=dst, send_sem=s_sem, recv_sem=r_sem,
            device_id=device, device_id_type=MESH,
        )

    def load(which, i):
        src, dst = ((tok_h, tok), (grad_h, grad))[which]
        return pltpu.make_async_copy(src.at[i], dst.at[i], s_load.at[which, i])

    load_rt = pltpu.make_async_copy(rt_h, rt_v, s_rt.at[0])
    load_rt.start()
    for i in range(IMG):
        load(0, i).start()

    barrier = pltpu.get_barrier_semaphore()
    for n in range(1, 16):
        pl.semaphore_signal(
            barrier, inc=1, device_id=in_dp(n // 4, (n // 2) % 2, n % 2), device_id_type=MESH
        )
    for k in range(1, 8):
        pl.semaphore_signal(barrier, inc=1, device_id=peer(k), device_id_type=MESH)

    load_rt.wait()
    rt = rt_v[...]

    def pre_in(n, carry):
        for u in range(4):
            load(0, 4 * n + u).wait()
            load(1, 4 * n + u).start()
        for u in range(4):
            i = 4 * n + u
            image = tok[i]
            logits = dot_nt(rt, image)
            e1 = jnp.exp(logits - jnp.max(logits, axis=1, keepdims=True))
            d = e1 / jnp.sum(e1, axis=1, keepdims=True)
            e0 = jnp.exp(logits - jnp.max(logits, axis=0, keepdims=True))
            c = e0 / jnp.sum(e0, axis=0, keepdims=True)
            disp[i] = d
            disp_b[i] = d.astype(BF)
            comb[i] = c
            stage[rows16(i)] = dot(d.astype(BF), image).astype(BF)
        return carry

    def pre_grad(n, carry):
        for u in range(4):
            load(1, 4 * n + u).wait()
        for u in range(4):
            i = 4 * n + u
            stage[rows16(i)] = dot(comb[i].astype(BF), grad[i]).astype(BF)
        return carry

    def wait_sent(ref, sem):
        remote(ref, ref, sem, sem, in_dp(1, 0)).wait_send()

    def wait_landed(ref, sem):
        remote(ref, ref, sem, sem, in_dp(1, 0)).wait_recv()

    def start_a2a(a):
        a2a_s[a] = permute_rows(by_slot, stage[...])
        for k in range(1, 8):
            remote(
                a2a_s.at[a, rows16(ex_of(k))], a2a_r.at[a, pl.ds(k * 16, 16)],
                s_a2a.at[a], r_a2a.at[a], peer(k),
            ).start()
        a2a_r[a, pl.ds(0, 16)] = a2a_s[a, rows16(ex)]

    lax.fori_loop(0, IMG // 4, pre_in, 0)
    pl.semaphore_wait(barrier, 22)
    start_a2a(0)
    lax.fori_loop(0, IMG // 4, pre_grad, 0)
    start_a2a(1)

    LAST = ((4, 5, 6, 7), (1, 3, 5, 7))

    def ag_copy(a, j, src_slot, dst_slot, dx, dz):
        sem = 0 if dst_slot in LAST[j] else dst_slot
        remote(
            rows.at[a, j, pl.ds(src_slot * 64, 64)], rows.at[a, j, pl.ds(dst_slot * 64, 64)],
            s_ag.at[a, j], r_ag.at[a, j, sem], in_dp(dx, dz),
        ).start()

    def ag_wait(a, j, slot):
        wait_landed(rows.at[a, j, pl.ds(slot * 64, 64)], r_ag.at[a, j, slot])

    def ag_own(a):
        wait_landed(a2a_r.at[a, pl.ds(16, 112)], r_a2a.at[a])
        ordered = permute_rows(by_expert, a2a_r[a])
        for j in range(2):
            rows[a, j, pl.ds(0, 64)] = ordered[j * 64 : j * 64 + 64]

    def ag_first(a):
        for j in range(2):
            ag_copy(a, j, 0, 2, 1, 0)
            ag_copy(a, j, 0, 1, 0, 1)
            ag_copy(a, j, 0, 6, 3, 0)

    def ag_second(a):
        ag_wait(a, 0, 1)
        ag_copy(a, 0, 1, 3, 1, 0)
        ag_copy(a, 0, 1, 7, 3, 0)
        for j in range(2):
            ag_wait(a, j, 2)
            ag_copy(a, j, 2, 4, 1, 0)
        ag_copy(a, 1, 2, 3, 0, 1)
        ag_wait(a, 1, 6)
        ag_copy(a, 1, 6, 7, 0, 1)

    def ag_third(a):
        ag_wait(a, 0, 3)
        ag_copy(a, 0, 3, 5, 1, 0)
        ag_wait(a, 1, 4)
        ag_copy(a, 1, 4, 5, 0, 1)

    def ag_end(a, j):
        wait_landed(rows.at[a, j, pl.ds(256, 256)], r_ag.at[a, j, 0])

    def project_in(j):
        for h in range(2):
            at = pl.ds(h * 256, 256)
            hid[j, at] = dot_nt(rows[0, j, at], w1[j])

    def project_grad(j):
        for h in range(2):
            at = pl.ds(h * 256, 256)
            act[1, j, at] = (dot_nt(rows[1, j, at], w2[j]) * hid[j, at]).astype(BF)

    def gelu(j):
        def step(n, carry):
            at = pl.ds(pl.multiple_of(n * 32, 32), 32)
            v = hid[j, at]
            half = 0.5 * (1.0 + lax.erf(v * root_half))
            act[0, j, at] = (v * half).astype(BF)
            hid[j, at] = half + v * jnp.exp(-0.5 * v * v) * inv_root_tau
            return carry

        lax.fori_loop(0, ROWS // 32, step, 0)

    def to_parts(o, w, j):
        def step(n, carry):
            at = pl.ds(pl.multiple_of(n * 256, 256), 256)
            total = dot(act[o, j], w[j, :, at]).astype(BF)
            parts[o, j, :, :, at] = total.reshape(8, 64, 256)
            return carry

        lax.fori_loop(0, D // 256, step, 0)

    dw = []

    def weight_grad(n, j):
        act_t[...] = act[1 - n, j].T

        def step(m, carry):
            at = pl.ds(pl.multiple_of(m * 256, 256), 256)
            total = dot(act_t[...], rows[n, j, :, at])
            dwk[n, j, :, at] = total[:HID]
            dws[n, j, :, at] = total[HID:].astype(BF)
            return carry

        lax.fori_loop(0, D // 256, step, 0)
        cp = remote(dws.at[n, j], dwr.at[n, j], s_dw.at[n, j], r_dw.at[n, j], in_dp(0, 0, 1))
        cp.start()
        dw.append((cp, n, j))

    FAR, NEAR = (3, 0), (4, 1)

    def rs_copy(o, j, piece, slot, count, land, sem, dx, dz):
        at = pl.ds(*piece)
        remote(
            parts.at[o, j, pl.ds(slot, count), at], rsb.at[o, j, pl.ds(land, count), at],
            s_rs.at[o, j], r_rs.at[o, j, sem + 8 * (piece[0] // 32)], in_dp(dx, dz),
        ).start()

    def part(o, j, piece, slot, count=1):
        return parts[o, j, pl.ds(slot, count), pl.ds(*piece)].astype(F32)

    def landed(o, j, piece, land, count, sem):
        ref = rsb.at[o, j, pl.ds(land, count), pl.ds(*piece)]
        wait_landed(ref, r_rs.at[o, j, sem + 8 * (piece[0] // 32)])
        return ref[...].astype(F32)

    def rs_begin(o, j):
        for piece, x_first in PIECES[o][j]:
            if x_first:
                for dz in (1, 0):
                    rs_copy(o, j, piece, 4 + dz, 1, dz, FAR[dz], 3, 0)
                for dz in (1, 0):
                    rs_copy(o, j, piece, 6 + dz, 1, 2 + dz, NEAR[dz], 1, 0)
            else:
                for dx in (2, 3, 1, 0):
                    rs_copy(o, j, piece, 2 * dx + 1, 1, dx, 3 + dx, 0, 1)

    def rs_add(o, j, piece, dx):
        total = part(o, j, piece, 2 * dx) + landed(o, j, piece, dx, 1, 3 + dx)
        parts[o, j, pl.ds(2 * dx, 1), pl.ds(*piece)] = total.astype(BF)

    def rs_far(o, j, piece):
        rs_add(o, j, piece, 2)
        rs_copy(o, j, piece, 4, 1, 4, 0, 3, 0)

    def rs_near(o, j, piece):
        rs_add(o, j, piece, 3)
        rs_copy(o, j, piece, 6, 1, 5, 1, 1, 0)
        rs_add(o, j, piece, 1)

    def rs_second(o, j, which=0):
        piece, x_first = PIECES[o][j][which]
        for slot, land, sem, last, last_sem in (
            ((3, 1, FAR[1], 5, NEAR[1]), (2, 0, FAR[0], 4, NEAR[0])) if x_first
            else ((2, 4, 0, 6, 1),)
        ):
            total = part(o, j, piece, slot) + landed(o, j, piece, land, 1, sem)
            parts[o, j, pl.ds(slot, 1), pl.ds(*piece)] = total.astype(BF)
            rs_copy(o, j, piece, slot, 1, last, last_sem, 3, 0)

    def ring_total(o, j, piece, dz):
        at = pl.ds(*piece)
        wait_landed(rsb.at[o, j, pl.ds(2, 2), at], r_rs.at[o, j, NEAR[dz] + 8 * (piece[0] // 32)])
        right, left = rsb[o, j, 2 + dz, at], rsb[o, j, 4 + dz, at]
        return part(o, j, piece, dz)[0] + right.astype(F32) + left.astype(F32)

    def rs_third(o, j, which=0):
        piece = PIECES[o][j][which][0]
        parts[o, j, 1, pl.ds(*piece)] = ring_total(o, j, piece, 1).astype(BF)
        rs_copy(o, j, piece, 1, 1, 6, 2, 0, 1)

    def rs_end(o, j):
        for piece, x_first in PIECES[o][j]:
            if x_first:
                total = ring_total(o, j, piece, 0) + landed(o, j, piece, 6, 1, 2)[0]
            else:
                both = landed(o, j, piece, 5, 2, 1)
                total = part(o, j, piece, 0)[0] + both[0] + both[1] + landed(o, j, piece, 0, 1, 3)[0]
            back_s[o, pl.ds(64 * j + piece[0], piece[1])] = total.astype(BF)

    def give_back(o):
        back_s[o] = permute_rows(by_peer, back_s[o])
        for k in range(1, 8):
            remote(
                back_s.at[o, pl.ds(k * 16, 16)], back_r.at[o, rows16(ex)],
                s_bk.at[o], r_bk.at[o], peer(k, -1),
            ).start()
        back_r[o, rows16(ex)] = back_s[o, pl.ds(0, 16)]

    def take_back(o):
        wait_landed(back_r.at[o, pl.ds(0, 112)], r_bk.at[o])
        return permute_rows(by_image, back_r[o])

    def hidden_step(j):
        ag_end(0, j)
        project_in(j)
        gelu(j)

    def grad_step(j):
        ag_end(1, j)
        project_grad(j)
        to_parts(1, w1, j)
        rs_begin(1, j)

    ag_own(0)
    ag_first(0)
    own_w, far_w = [], []
    for n, (src, dst) in enumerate(((w1_h, w1), (w2_h, w2))):
        for j in range(2):
            own_w.append(pltpu.make_async_copy(
                src.at[j], dst.at[j, pl.ds(0, HID)], s_loc.at[n, j]))
            far_w.append(remote(
                src.at[j], dst.at[j, pl.ds(HID, HID)], s_w.at[n, j], s_wr.at[n, j],
                in_dp(0, 0, 1)))
    for cp in own_w + far_w:
        cp.start()
    ag_own(1)
    ag_second(0)
    ag_first(1)
    ag_third(0)
    for cp in own_w:
        cp.wait()
    for cp in far_w:
        cp.wait_recv()
    ag_second(1)
    hidden_step(0)
    to_parts(0, w2, 0)
    rs_begin(0, 0)
    hidden_step(1)
    ag_third(1)
    to_parts(0, w2, 1)
    rs_begin(0, 1)
    grad_step(0)
    rs_second(0, 1)
    grad_step(1)
    weight_grad(1, 0)
    weight_grad(1, 1)
    weight_grad(0, 0)
    rs_second(1, 0, 1)
    rs_far(0, 0, WHOLE)
    rs_near(0, 0, WHOLE)
    rs_third(0, 1)
    rs_second(1, 1)
    rs_second(0, 0)
    rs_far(1, 0, TOP)
    weight_grad(0, 1)
    rs_near(1, 0, TOP)
    rs_third(1, 0, 1)
    rs_second(1, 0, 0)
    rs_end(0, 1)
    rs_third(1, 1)
    rs_end(0, 0)
    give_back(0)
    rs_end(1, 0)
    rs_end(1, 1)
    give_back(1)
    sb[0] = take_back(0)

    def comb_side(n, carry):
        for u in range(4):
            i = 4 * n + u
            g = dot_nt(sb[0, rows16(i)], grad[i])
            c = comb[i]
            comb[i] = c * (g - jnp.sum(c * g, axis=0, keepdims=True))
        return carry

    lax.fori_loop(0, IMG // 4, comb_side, 0)

    sb[1] = take_back(1)
    small = [
        pltpu.make_async_copy(sb.at[1], back_h, s_rt.at[0]),
        pltpu.make_async_copy(disp_b, disp_h, s_rt.at[1]),
        pltpu.make_async_copy(lg, lg_h, s_rt.at[2]),
    ]

    def disp_side(n, total):
        for u in range(4):
            i = 4 * n + u
            g = dot_nt(sb[1, rows16(i)], tok[i])
            d = disp[i]
            lg[i] = (comb[i] + d * (g - jnp.sum(d * g, axis=1, keepdims=True))).astype(BF)
        for u in range(4):
            i = 4 * n + u
            total = total + dot(lg[i], tok[i])
        return total

    term = lax.fori_loop(0, IMG // 4, disp_side, jnp.zeros((S, D), F32))
    for p in range(8):
        lane = 384 * (p // 2)
        width = min(384, D - lane)
        arp[p, :, pl.ds(0, width)] = term[8 * (p % 2) : 8 * (p % 2) + 8, lane : lane + width]
        if width < 384:
            arp[p, :, pl.ds(width, 384 - width)] = jnp.zeros((8, 384 - width), F32)

    for k in range(1, 8):
        remote(arp.at[ex_of(k)], arr.at[k], s_ar.at[0], r_ar.at[0], peer(k)).start()
    for cp in small:
        cp.start()
    for n in range(2):
        wait_sent(a2a_s.at[n, pl.ds(0, 112)], s_a2a.at[n])
        wait_sent(back_s.at[n, pl.ds(0, 112)], s_bk.at[n])
        for j in range(2):
            wait_sent(rows.at[n, j, pl.ds(64, 448)], s_ag.at[n, j])
            wait_sent(rsb.at[n, j], s_rs.at[n, j])
    wait_landed(arr.at[pl.ds(1, 7)], r_ar.at[0])
    total = arp[ex]
    for k in range(1, 8):
        total = total + arr[k]
    ars[0] = total
    for n in range(1, 16):
        remote(
            ars.at[0], arg.at[dp], s_ar.at[1], r_ar.at[1], in_dp(n // 4, (n // 2) % 2, n % 2)
        ).start()
    arg[dp] = total
    for cp in far_w:
        cp.wait_send()

    for cp, n, j in dw:
        cp.wait()
        dws[n, j] = (dwk[n, j] + dwr[n, j].astype(F32)).astype(BF)
        out = (dw1_h, dw2_h)[n]
        pltpu.make_async_copy(dws.at[n, j], out.at[j], s_dwo.at[n, j]).start()

    wait_landed(arg.at[pl.ds(0, 15)], r_ar.at[1])
    total = arg[0]
    for n in range(1, 16):
        total = total + arg[n]
    ars[1] = total
    for k in range(1, 8):
        remote(ars.at[1], arf.at[ex], s_ar.at[2], r_ar.at[2], peer(k)).start()
    arf[ex] = total
    wait_sent(arp.at[pl.ds(0, 7)], s_ar.at[0])
    wait_sent(arg.at[pl.ds(0, 15)], s_ar.at[1])
    for cp in small:
        cp.wait()
    for n in range(2):
        for j in range(2):
            out = (dw1_h, dw2_h)[n]
            pltpu.make_async_copy(dws.at[n, j], out.at[j], s_dwo.at[n, j]).wait()
    wait_landed(arf.at[pl.ds(0, 7)], r_ar.at[2])
    for p in range(8):
        lane = 384 * (p // 2)
        width = min(384, D - lane)
        router_out[pl.ds(8 * (p % 2), 8), pl.ds(lane, width)] = arf[p, :, pl.ds(0, width)]
    wait_sent(arf.at[pl.ds(0, 7)], s_ar.at[2])


def token_kernel(
    rt_h, router_h, back_h, disp_h, lg_h, dw1_in, dw2_in,
    token_grad_h, router_out, dw1_h, dw2_h,
    rt_v, router_v, back_v, disp_v, lg_v, tgo, dwv, s_small, s_out, s_in, s_dw,
):
    small = [
        pltpu.make_async_copy(src, dst, s_small.at[n])
        for n, (src, dst) in enumerate((
            (rt_h, rt_v), (back_h, back_v), (disp_h, disp_v), (lg_h, lg_v), (router_h, router_v)))
    ]
    reads, writes = [], []
    for n, (src, dst) in enumerate(((dw1_in, dw1_h), (dw2_in, dw2_h))):
        reads.append(pltpu.make_async_copy(src, dwv.at[n], s_in.at[n]))
        writes.append(pltpu.make_async_copy(dwv.at[n], dst, s_dw.at[n]))
    router_write = pltpu.make_async_copy(router_v, router_out, s_small.at[5])
    for cp in small + reads:
        cp.start()
    for cp in small:
        cp.wait()
    router_write.start()
    for i in range(IMG):
        left = jnp.concatenate([disp_v[i], lg_v[i]], axis=0)
        right = jnp.concatenate([back_v[pl.ds(i * 16, 16)], rt_v[...]], axis=0)
        tgo[i] = dot_tn(left, right).astype(BF)
        cp = pltpu.make_async_copy(tgo.at[i], token_grad_h.at[i], s_out.at[i])
        cp.start()
        writes.append(cp)
        if i in (1, 3):
            reads[i // 2].wait()
            writes[i // 2].start()
    for cp in writes + [router_write]:
        cp.wait()


def shards(tokens, router, weight_in, weight_out, out_grad):
    any_space = pl.BlockSpec(memory_space=pl.ANY)
    vmem = pl.BlockSpec(memory_space=pltpu.VMEM)
    dma = pltpu.SemaphoreType.DMA
    V = pltpu.VMEM
    router_t = router.T
    router_grad, back, disp_half, grad_logit, dw1, dw2 = pl.pallas_call(
        kernel,
        name="soft_moe",
        out_shape=(
            jax.ShapeDtypeStruct((S, D), F32),
            jax.ShapeDtypeStruct((128, D), BF),
            jax.ShapeDtypeStruct((IMG, S, M), BF),
            jax.ShapeDtypeStruct((IMG, S, M), BF),
            jax.ShapeDtypeStruct((2, HID, D), BF),
            jax.ShapeDtypeStruct((2, HID, D), BF),
        ),
        in_specs=[any_space] * 5,
        out_specs=(vmem,) + (any_space,) * 5,
        scratch_shapes=[
            V((IMG, M, D), BF), V((IMG, M, D), BF),
            V((2, HID2, D), BF), V((2, HID2, D), BF),
            V((IMG, S, M), F32), V((IMG, S, M), F32),
            V((128, D), BF), V((2, 128, D), BF), V((2, 128, D), BF),
            V((2, 2, ROWS, D), BF), V((2, 2, 8, 64, D), BF),
            V((2, 2, 7, 64, D), BF),
            V((2, ROWS, HID2), F32), V((2, 2, ROWS, HID2), BF), V((HID2, ROWS), BF),
            V((2, 2, HID, D), F32), V((2, 2, HID, D), BF), V((2, 2, HID, D), BF),
            V((2, 128, D), BF), V((2, 128, D), BF),
            V((2, 128, D), BF),
            V((8, 8, 384), F32), V((8, 8, 384), F32), V((2, 8, 384), F32),
            V((16, 8, 384), F32), V((8, 8, 384), F32),
            V((S, D), BF), V((IMG, S, M), BF), V((IMG, S, M), BF),
            dma((2, IMG)), dma((2, 2)), dma((2, 2)), dma((2,)), dma((2,)),
            dma((2, 2)), dma((2, 2, 8)), dma((2, 2)), dma((2, 2, 16)),
            dma((2,)), dma((2,)), dma((2, 2)), dma((2, 2)), dma((2, 2)),
            dma((3,)), dma((3,)), dma((2, 2)), dma((3,)),
        ],
        compiler_params=pltpu.CompilerParams(
            collective_id=0, has_side_effects=True, vmem_limit_bytes=62 * 2**20
        ),
    )(tokens, out_grad, router_t, jnp.swapaxes(weight_in, 1, 2), weight_out)
    token_grad, router_grad, dw1, dw2 = pl.pallas_call(
        token_kernel,
        name="token_grad",
        out_shape=(
            jax.ShapeDtypeStruct((IMG, M, D), BF),
            jax.ShapeDtypeStruct((S, D), F32),
            jax.ShapeDtypeStruct((2, HID, D), BF),
            jax.ShapeDtypeStruct((2, HID, D), BF),
        ),
        in_specs=[any_space] * 7,
        out_specs=(any_space,) * 4,
        scratch_shapes=[
            V((S, D), BF), V((S, D), F32), V((128, D), BF), V((IMG, S, M), BF), V((IMG, S, M), BF),
            V((IMG, M, D), BF), V((2, 2, HID, D), BF), dma((6,)), dma((IMG,)), dma((2,)), dma((2,)),
        ],
        compiler_params=pltpu.CompilerParams(vmem_limit_bytes=62 * 2**20),
    )(router_t, router_grad, back, disp_half, grad_logit, dw1, dw2)
    return token_grad, router_grad.T, jnp.swapaxes(dw1, 1, 2), dw2


def solution(mesh):
    in_specs = (
        P(("dp", "expert"), None, None),
        P(),
        P("expert", None, "dp"),
        P("expert", "dp", None),
        P(("dp", "expert"), None, None),
    )
    out_specs = (
        P(("dp", "expert"), None, None),
        P(),
        P("expert", None, "dp"),
        P("expert", "dp", None),
    )
    return jax.shard_map(shards, mesh=mesh, in_specs=in_specs, out_specs=out_specs, check_vma=False)
```
